128 devices in a mesh: dp: 8 (over y, core), ctx: 16 (over z, x).
Axes of the slice: x: 4, y: 4, z: 4, core: 2. Of those that a mesh axis runs over, the one named last changes fastest.
Arguments:
- queries: bfloat16 [16384, 2048], P(('dp', 'ctx')), may hold values from -6 to 6
- key_rows: bfloat16 [16384, 2048], P(('dp', 'ctx')), may hold values from -6 to 6
- value_rows: bfloat16 [16384, 2048], P(('dp', 'ctx')), may hold values from -6 to 6
- hidden_in: bfloat16 [16384, 2304], P(('dp', 'ctx')), may hold values from -24 to 24
- beta_weight: bfloat16 [2304, 16], replicated, may hold values from -0.125 to 0.125
- log_gate: float32 [16, 16384], P(None, ('dp', 'ctx')), may hold values from -1 to 0
- out_grad: bfloat16 [16384, 2048], P(('dp', 'ctx')), may hold values from -24 to 24
- lengths: int32 [8, 4], P('dp'), may hold values from 1 to 1024, 2048 in all within a row
- rewards: float32 [32], replicated, may hold values from -6 to 6
- prompts: int32 [32], replicated, may hold values from 0 to 7
Outputs:
- query_grad: bfloat16 [16384, 2048], P(('dp', 'ctx'))
- key_grad: bfloat16 [16384, 2048], P(('dp', 'ctx'))
- value_grad: bfloat16 [16384, 2048], P(('dp', 'ctx'))
- gate_grad: float32 [16, 16384], P(None, ('dp', 'ctx'))
- beta_weight_grad: float32 [2304, 16], P(('dp', 'ctx'))
The draws below stay inside these ranges and needn't reach their ends.
Inputs may be any that keep to these rules, and one draw needn't show every extreme that they name: `lengths`: each row sums to 2048; its largest entry is exactly 1024.
All inputs are finite; a program needn't handle non-finite values.
Results may differ from the reference program's by a relative error of at most 0.001.
Values sent between devices are 32-bit elements; how exact they have to be, the bound alone decides.
No kernel may reach another device: no remote copies, remote signals or barrier semaphores. Data moves between devices by JAX's collectives and lax.ppermute only.
A program may use at most 128 MiB of HBM per device.

```python
import math
import jax
import jax.numpy as jnp
import numpy as np
from jax import lax

D = 2304
HALF_HEADS = 16
HEAD_DIM = 128
BLOCK = 64
TOK_DEV = 128
ROLL = 4
GROUP_TOKENS = 2048
TOTAL_TOKENS = 16384
ROLLOUTS = 32
PROMPTS = 8
N_DP = 8


def draw_log_gate(key, part):
    key_vectors = jax.random.split(key, 7)
    fast_share = 0.5
    fast = jax.random.uniform(key_vectors[0], (HALF_HEADS, 1)) < fast_share
    fast_rate = jnp.exp(jax.random.uniform(key_vectors[1], (HALF_HEADS, 1), minval=math.log(1.0 / 50.0), maxval=math.log(1.0 / 30.0)))
    slow_rate = jnp.exp(jax.random.uniform(key_vectors[2], (HALF_HEADS, 1), minval=math.log(0.05), maxval=math.log(0.3))) / GROUP_TOKENS
    decay_speed = jnp.where(fast, fast_rate, slow_rate)
    block_multiplier = jnp.exp(jax.random.uniform(key_vectors[3], (HALF_HEADS, TOTAL_TOKENS // TOK_DEV, 1), minval=math.log(0.5), maxval=math.log(2.0)))
    block_multiplier = jnp.broadcast_to(block_multiplier, (HALF_HEADS, TOTAL_TOKENS // TOK_DEV, TOK_DEV)).reshape(HALF_HEADS, TOTAL_TOKENS)
    token_multiplier = jnp.exp(jax.random.uniform(key_vectors[4], (HALF_HEADS, TOTAL_TOKENS), minval=math.log(0.5), maxval=math.log(2.0)))
    spike_position = jax.random.uniform(key_vectors[5], (1, TOTAL_TOKENS)) < 3.0 / GROUP_TOKENS
    spike_magnitude = jax.random.uniform(key_vectors[6], (HALF_HEADS, TOTAL_TOKENS), minval=math.log(0.5), maxval=math.log(0.8))
    return (-decay_speed * block_multiplier * token_multiplier + jnp.where(spike_position, spike_magnitude, 0.0)).astype(jnp.float32)


def plant(entries, own_key, low, high):
    longest = entries.shape.index(max(entries.shape))
    spots = []
    for shift in (0, 1):
        where = [jax.random.randint(jax.random.fold_in(own_key, axis), (), 0, length) for axis, length in enumerate(entries.shape)]
        where[longest] = (where[longest] + shift) % entries.shape[longest]
        spots.append(tuple(where))
    return entries.at[spots[0]].set(low).at[spots[1]].set(high)


def with_spikes(array, key, source, target, shards_of, factor):
    owner, partner = [(jnp.arange(array.shape[position]) // (array.shape[position] // shards_of)).reshape([-1 if axis == position else 1 for axis in range(array.ndim)]) for position in (source, target)]
    chosen = jax.random.permutation(key, shards_of)[partner]
    strong = (owner == chosen) | (owner == (partner + shards_of // 2) % shards_of)
    return jnp.where(strong, factor * array, array)


def block_levels(stream_key, shape, cuts, low, high):
    loudness, own = 1.0, jax.random.fold_in(stream_key, 6)
    for position, shards_of in cuts:
        heights = jnp.exp(jax.random.uniform(jax.random.fold_in(own, position), (shards_of,), jnp.float32, low / len(cuts), high / len(cuts)))
        loudness = loudness * jnp.repeat(heights, shape[position] // shards_of).reshape([-1 if axis == position else 1 for axis in range(len(shape))])
    return loudness


def split_up(count, total, bound, skew):
    weights = [(1 << 20) // math.isqrt(rank ** skew) + 1 for rank in range(2, count + 1)]
    surplus, holding = total - bound - (count - 1), [1] * (count - 1)
    while surplus > 0:
        movable = [i for i in range(count - 1) if holding[i] < bound]
        pool, left = sum([weights[i] for i in movable]), surplus
        for i in movable:
            extra = min(bound - holding[i], max(1, left * weights[i] // pool), surplus)
            holding[i] = holding[i] + extra
            surplus = surplus - extra
    return np.array([bound] + holding)


def ragged(own_key, number_of, total, limit, lean):
    if number_of == 2:
        one = jax.random.randint(own_key, (), max(1, total - limit), min(limit, total - 1) + 1)
        return jnp.stack([one, total - one])
    sizes = jnp.asarray(split_up(number_of, total, limit, lean), jnp.int32)
    twos = (number_of - 1) // 2
    donor, taker = sizes[1:1 + 2 * twos:2], sizes[2:2 + 2 * twos:2]
    slack = jnp.minimum(donor - 1, limit - taker)
    shifted = jax.random.randint(jax.random.fold_in(own_key, 1), (twos,), 0, 1 << 20) % (slack + 1)
    sizes = sizes.at[1:1 + 2 * twos:2].set(donor - shifted).at[2:2 + 2 * twos:2].set(taker + shifted)
    return sizes[jax.random.permutation(jax.random.fold_in(own_key, 2), number_of)]


def gaussian(key, dims, scale, reach, cuts=(), held_as=jnp.bfloat16):
    drawn = jax.random.normal(key, dims, jnp.float32) * scale
    if len(cuts) > 0:
        drawn = block_levels(key, dims, cuts, -0.22, 0.18) * drawn
    return jnp.clip(drawn, min=-reach, max=reach).astype(held_as)


def bell_draw_with(rng, shape, scale, reach, cuts, heavy, kind=jnp.bfloat16):
    values = scale * jax.random.normal(rng, shape, jnp.float32)
    if cuts:
        values = values * block_levels(rng, shape, cuts, -0.22, 0.18)
    return jnp.clip(with_spikes(values, jax.random.fold_in(rng, 3), *heavy), -reach, reach).astype(kind)


def setup_inputs(seed: int = 0) -> dict:
    seeds = jax.random.split(jax.random.key(seed), 11)
    return {
        "queries": gaussian(seeds[0], (TOTAL_TOKENS, HALF_HEADS * HEAD_DIM), 1.0, 6.0, ((0, 128),)),
        "key_rows": gaussian(seeds[1], (TOTAL_TOKENS, HALF_HEADS * HEAD_DIM), 1.0, 6.0, ((0, 128),)),
        "value_rows": gaussian(seeds[2], (TOTAL_TOKENS, HALF_HEADS * HEAD_DIM), 1.0, 6.0, ((0, 128),)),
        "hidden_in": bell_draw_with(seeds[3], (TOTAL_TOKENS, D), 1.0, 24.0, ((0, 128),), (0, 1, 128, 5.5)),
        "beta_weight": gaussian(seeds[4], (D, HALF_HEADS), D ** -0.5, 0.125),
        "log_gate": draw_log_gate(jax.random.fold_in(seeds[10], 71), 0),
        "out_grad": gaussian(seeds[6], (TOTAL_TOKENS, HALF_HEADS * HEAD_DIM), 4.0, 24.0, ((0, 128),)),
        "lengths": jax.vmap(lambda own: ragged(own, ROLL, GROUP_TOKENS, GROUP_TOKENS // 2, 2))(jax.random.split(seeds[7], N_DP)).reshape((N_DP, ROLL)).astype(jnp.int32),
        "rewards": gaussian(seeds[8], (ROLLOUTS,), 1.0, 6.0, (), jnp.float32),
        "prompts": plant(jax.random.randint(seeds[9], (ROLLOUTS,), 0, PROMPTS), jax.random.fold_in(seeds[9], 1), 0, PROMPTS - 1).astype(jnp.int32),
    }


highest = lax.Precision.HIGHEST

def unit_rows(rows):
    return rows * lax.rsqrt(lax.optimization_barrier(jnp.sum(rows * rows, axis=-1, keepdims=True)) + 1e-06)

def unit_inverse(lower_part):
    size = lower_part.shape[-1]
    nilpotent = -lower_part
    total = jnp.eye(size, dtype=jnp.float32) + nilpotent
    power = nilpotent
    for level in range(max(1, (size - 1).bit_length()) - 1):
        power = jnp.einsum('nhij,nhjk->nhik', power, power, precision=highest)
        total = total + jnp.einsum('nhij,nhjk->nhik', total, power, precision=highest)
    return total

def block_terms(queries, key_rows, value_rows, beta, gate_log, starts):
    size = queries.shape[2]
    row_ids = lax.broadcasted_iota(jnp.int32, (size, size), 0)
    col_ids = lax.broadcasted_iota(jnp.int32, (size, size), 1)
    gamma = jnp.cumsum(gate_log, axis=-1)
    count = jnp.cumsum(starts, axis=-1)
    linked = (count[:, :, None] == count[:, None, :]) & (row_ids >= col_ids)
    linked = linked[:, None, :, :]
    spread = gamma[..., :, None] - gamma[..., None, :]
    decay = jnp.where(linked, jnp.exp(jnp.where(linked, spread, 0.0)), 0.0)
    head_decay = jnp.where(count == 0.0, 1.0, 0.0)[:, None, :] * jnp.exp(gamma)
    tail_decay = decay[..., size - 1, :]
    key_key = jnp.einsum('nhik,nhjk->nhij', key_rows, key_rows, precision=highest)
    lower_part = jnp.where(row_ids > col_ids, beta[..., :, None] * decay * key_key, 0.0)
    inverse = unit_inverse(lower_part)
    rhs_value = beta[..., None] * value_rows
    rhs_key = (beta * head_decay)[..., None] * key_rows
    u_zero = jnp.einsum('nhij,nhjv->nhiv', inverse, rhs_value, precision=highest)
    z_rows = jnp.einsum('nhij,nhjk->nhik', inverse, rhs_key, precision=highest)
    mixing = decay * jnp.einsum('nhik,nhjk->nhij', queries, key_rows, precision=highest)
    out_zero = jnp.einsum('nhij,nhjv->nhiv', mixing, u_zero, precision=highest)
    carry_q = head_decay[..., None] * queries - jnp.einsum('nhij,nhjk->nhik', mixing, z_rows, precision=highest)
    weighted = tail_decay[..., None] * key_rows
    state_zero = jnp.einsum('nhcv,nhck->nhvk', u_zero, weighted, precision=highest)
    identity = jnp.eye(key_rows.shape[-1], dtype=jnp.float32)
    transfer = head_decay[..., size - 1][..., None, None] * identity - jnp.einsum('nhck,nhcj->nhkj', z_rows, weighted, precision=highest)
    return (out_zero, carry_q, state_zero, transfer)

def run_blocks(out_zero, carry_q, state_zero, transfer, state_in):

    def advance(state, pieces):
        piece_out, piece_q, piece_state, piece_map = pieces
        result = piece_out + jnp.einsum('hck,hvk->hcv', piece_q, state, precision=highest)
        updated = jnp.einsum('hvk,hkj->hvj', state, piece_map, precision=highest) + piece_state
        return (updated, result)
    final, outputs = lax.scan(advance, state_in, (out_zero, carry_q, state_zero, transfer))
    return (outputs, final)

def segment_terms(query_f, key_f, value_f, logits, gate_log, starts):
    token_count, heads = logits.shape
    blocks = token_count // BLOCK

    def split(rows):
        return rows.reshape(blocks, BLOCK, heads, -1).transpose(0, 2, 1, 3)
    beta = jax.nn.sigmoid(logits).reshape(blocks, BLOCK, heads).transpose(0, 2, 1)
    gates = gate_log.reshape(heads, blocks, BLOCK).transpose(1, 0, 2)
    return block_terms(unit_rows(split(query_f)), unit_rows(split(key_f)), split(value_f), beta, gates, starts.reshape(blocks, BLOCK))

def output_from_terms(terms, state_in):
    outputs, final = run_blocks(terms[0], terms[1], terms[2], terms[3], state_in)
    token_count = outputs.shape[0] * outputs.shape[2]
    return (outputs.transpose(0, 2, 1, 3).reshape(token_count, -1), final)

def segment_output(query_f, key_f, value_f, logits, gate_log, starts, state_in):
    return output_from_terms(segment_terms(query_f, key_f, value_f, logits, gate_log, starts), state_in)

def token_plan(row_lengths, positions):
    ends = jnp.cumsum(row_lengths)
    begins = ends - row_lengths
    starts = jnp.any(positions[:, None] == begins[None, :], axis=1).astype(jnp.float32)
    member = ((positions[:, None] >= begins[None, :]) & (positions[:, None] < ends[None, :])).astype(jnp.float32)
    return (starts, member)

def advantages(rewards, prompts):
    same = (prompts[:, None] == prompts[None, :]).astype(jnp.float32)
    return rewards - lax.optimization_barrier(jnp.sum(same * rewards[None, :], axis=1)) / lax.optimization_barrier(jnp.sum(same, axis=1))

def reference(queries, key_rows, value_rows, hidden_in, beta_weight, log_gate, out_grad, lengths, rewards, prompts):
    roll_weight = advantages(rewards, prompts).reshape(N_DP, ROLL) * GROUP_TOKENS / (ROLL * lengths.astype(jnp.float32))
    positions = jnp.arange(GROUP_TOKENS, dtype=jnp.int32)
    starts, member = jax.vmap(token_plan, (0, None))(lengths, positions)
    token_weight = lax.optimization_barrier(jnp.sum(member * roll_weight[:, None, :], axis=-1)).reshape(TOTAL_TOKENS)
    cotangent = out_grad.astype(jnp.float32) * token_weight[:, None]
    logits = jnp.dot(hidden_in, beta_weight, preferred_element_type=jnp.float32)
    width = HALF_HEADS * HEAD_DIM
    zero_state = jnp.zeros((HALF_HEADS, HEAD_DIM, HEAD_DIM), jnp.float32)

    def one_group(pieces):
        query_f, key_f, value_f, group_logits, group_gates, group_starts, group_cot = pieces

        def forward(a_rows, b_rows, c_rows, d_rows, e_rows):
            return segment_output(a_rows, b_rows, c_rows, d_rows, e_rows, group_starts, zero_state)[0]
        primal, backward = jax.vjp(forward, query_f, key_f, value_f, group_logits, group_gates)
        return backward(group_cot)
    grads = lax.map(one_group, (queries.astype(jnp.float32).reshape(N_DP, GROUP_TOKENS, width), key_rows.astype(jnp.float32).reshape(N_DP, GROUP_TOKENS, width), value_rows.astype(jnp.float32).reshape(N_DP, GROUP_TOKENS, width), logits.reshape(N_DP, GROUP_TOKENS, HALF_HEADS), log_gate.reshape(HALF_HEADS, N_DP, GROUP_TOKENS).transpose(1, 0, 2), starts, cotangent.reshape(N_DP, GROUP_TOKENS, width)))
    query_grad = grads[0].reshape(TOTAL_TOKENS, width).astype(jnp.bfloat16)
    key_grad = grads[1].reshape(TOTAL_TOKENS, width).astype(jnp.bfloat16)
    value_grad = grads[2].reshape(TOTAL_TOKENS, width).astype(jnp.bfloat16)
    logit_grad = grads[3].reshape(TOTAL_TOKENS, HALF_HEADS)
    gate_grad = grads[4].transpose(1, 0, 2).reshape(HALF_HEADS, TOTAL_TOKENS)
    beta_weight_grad = jnp.dot(hidden_in.astype(jnp.float32).T, logit_grad, precision=highest, preferred_element_type=jnp.float32)
    return (query_grad, key_grad, value_grad, gate_grad, beta_weight_grad)
```

```python
import jax
import jax.numpy as jnp
from jax import lax
from jax.sharding import PartitionSpec as P

BLOCK = 64


highest = lax.Precision.HIGHEST


def from_behind(x, axis, by):
    length = lax.axis_size(axis)
    pairs = [(i, i + by) for i in range(length) if 0 <= i + by < length]
    return lax.ppermute(x, axis, pairs)


def unit_rows(rows):
    return rows * lax.rsqrt(jnp.sum(rows * rows, axis=-1, keepdims=True) + 1e-06)


def unit_inverse(lower_part):
    size = lower_part.shape[-1]
    nilpotent = -lower_part
    total = jnp.eye(size, dtype=jnp.float32) + nilpotent
    power = nilpotent
    for level in range(max(1, (size - 1).bit_length()) - 1):
        power = jnp.einsum("nhij,nhjk->nhik", power, power, precision=highest)
        total = total + jnp.einsum("nhij,nhjk->nhik", total, power, precision=highest)
    return total


def block_terms(queries, key_rows, value_rows, beta, gate_log, starts):
    size = queries.shape[2]
    row_ids = lax.broadcasted_iota(jnp.int32, (size, size), 0)
    col_ids = lax.broadcasted_iota(jnp.int32, (size, size), 1)
    upto = (row_ids <= col_ids).astype(jnp.float32)
    gamma = jnp.einsum("nhi,ij->nhj", gate_log, upto, precision=highest)
    count = jnp.einsum("ni,ij->nj", starts, upto, precision=highest)
    linked = (count[:, :, None] == count[:, None, :]) & (row_ids >= col_ids)
    linked = linked[:, None, :, :]
    spread = gamma[..., :, None] - gamma[..., None, :]
    decay = jnp.where(linked, jnp.exp(jnp.where(linked, spread, 0.0)), 0.0)
    head_decay = jnp.where(count == 0.0, 1.0, 0.0)[:, None, :] * jnp.exp(gamma)
    tail_decay = decay[..., size - 1, :]
    key_key = jnp.einsum("nhik,nhjk->nhij", key_rows, key_rows, precision=highest)
    lower_part = jnp.where(row_ids > col_ids, beta[..., :, None] * decay * key_key, 0.0)
    inverse = unit_inverse(lower_part)
    rhs_value = beta[..., None] * value_rows
    rhs_key = (beta * head_decay)[..., None] * key_rows
    u_zero = jnp.einsum("nhij,nhjv->nhiv", inverse, rhs_value, precision=highest)
    z_rows = jnp.einsum("nhij,nhjk->nhik", inverse, rhs_key, precision=highest)
    mixing = decay * jnp.einsum("nhik,nhjk->nhij", queries, key_rows, precision=highest)
    out_zero = jnp.einsum("nhij,nhjv->nhiv", mixing, u_zero, precision=highest)
    carry_q = head_decay[..., None] * queries - jnp.einsum(
        "nhij,nhjk->nhik", mixing, z_rows, precision=highest
    )
    weighted = tail_decay[..., None] * key_rows
    state_zero = jnp.einsum("nhcv,nhck->nhvk", u_zero, weighted, precision=highest)
    identity = jnp.eye(key_rows.shape[-1], dtype=jnp.float32)
    transfer = head_decay[..., size - 1][..., None, None] * identity - jnp.einsum(
        "nhck,nhcj->nhkj", z_rows, weighted, precision=highest
    )
    return (out_zero, carry_q, state_zero, transfer)


def run_blocks(out_zero, carry_q, state_zero, transfer, state_in):

    def advance(state, pieces):
        piece_out, piece_q, piece_state, piece_map = pieces
        result = piece_out + jnp.einsum("hck,hvk->hcv", piece_q, state, precision=highest)
        updated = jnp.einsum("hvk,hkj->hvj", state, piece_map, precision=highest) + piece_state
        return (updated, result)

    final, outputs = lax.scan(advance, state_in, (out_zero, carry_q, state_zero, transfer))
    return (outputs, final)


def segment_terms(query_f, key_f, value_f, logits, gate_log, starts):
    token_count, heads = logits.shape
    blocks = token_count // BLOCK

    def split(rows):
        return rows.reshape(blocks, BLOCK, heads, -1).transpose(0, 2, 1, 3)

    beta = jax.nn.sigmoid(logits).reshape(blocks, BLOCK, heads).transpose(0, 2, 1)
    gates = gate_log.reshape(heads, blocks, BLOCK).transpose(1, 0, 2)
    return block_terms(
        unit_rows(split(query_f)),
        unit_rows(split(key_f)),
        split(value_f),
        beta,
        gates,
        starts.reshape(blocks, BLOCK),
    )


def output_from_terms(terms, state_in):
    outputs, final = run_blocks(terms[0], terms[1], terms[2], terms[3], state_in)
    token_count = outputs.shape[0] * outputs.shape[2]
    return (outputs.transpose(0, 2, 1, 3).reshape(token_count, -1), final)


def segment_map(terms, zero_state):

    def compose_step(carry, pieces):
        linear, offset = carry
        piece_state, piece_map = pieces
        linear = jnp.einsum("hij,hjk->hik", linear, piece_map, precision=highest)
        offset = jnp.einsum("hvk,hkj->hvj", offset, piece_map, precision=highest) + piece_state
        return ((linear, offset), None)

    start_map = jnp.broadcast_to(jnp.eye(zero_state.shape[-1], dtype=jnp.float32), zero_state.shape)
    result, unused = lax.scan(compose_step, (start_map, zero_state), (terms[2], terms[3]))
    return result


def token_plan(row_lengths, positions):
    slots = jnp.arange(row_lengths.shape[0])
    ends = jnp.sum(jnp.where(slots[:, None] <= slots[None, :], row_lengths[:, None], 0), axis=0)
    begins = ends - row_lengths
    starts = jnp.any(positions[:, None] == begins[None, :], axis=1).astype(jnp.float32)
    member = (
        (positions[:, None] >= begins[None, :]) & (positions[:, None] < ends[None, :])
    ).astype(jnp.float32)
    return (starts, member)


def advantages(rewards, prompts):
    same = (prompts[:, None] == prompts[None, :]).astype(jnp.float32)
    return rewards - jnp.sum(same * rewards[None, :], axis=1) / jnp.sum(same, axis=1)


def chains(linear, offset, local_back):
    def step(state, pieces):
        piece_map, piece_add = pieces
        return (jnp.dot(state, piece_map, precision=highest) + piece_add, state)

    zero = jnp.zeros_like(offset[0])
    state_in = lax.scan(step, zero, (linear, offset))[1]
    flipped = jnp.swapaxes(linear, 1, 2)
    end_grad = lax.scan(step, zero, (flipped, local_back), reverse=True)[1]
    return (state_in, end_grad)


def to_owners(x):
    return lax.all_to_all(x, "ctx", 0, 0, tiled=True)


def local(
    queries,
    key_rows,
    value_rows,
    hidden_in,
    beta_weight,
    log_gate,
    out_grad,
    lengths,
    rewards,
    prompts,
):
    token_count = queries.shape[0]
    heads = beta_weight.shape[1]
    width = queries.shape[1] // heads
    ctx_count = lax.axis_size("ctx")
    roll_count = lengths.shape[1]
    group_tokens = token_count * ctx_count
    positions = lax.axis_index("ctx") * token_count + jnp.arange(token_count, dtype=jnp.int32)
    starts, member = token_plan(lengths[0], positions)
    own_advantage = lax.dynamic_slice_in_dim(
        advantages(rewards, prompts), lax.axis_index("dp") * roll_count, roll_count
    )
    roll_weight = own_advantage * group_tokens / (roll_count * lengths[0].astype(jnp.float32))
    token_weight = jnp.sum(member * roll_weight[None, :], axis=-1)
    cotangent = out_grad.astype(jnp.float32) * token_weight[:, None]
    logits = jnp.dot(hidden_in, beta_weight, preferred_element_type=jnp.float32)
    query_f = queries.astype(jnp.float32)
    key_f = key_rows.astype(jnp.float32)
    value_f = value_rows.astype(jnp.float32)
    zero_state = jnp.zeros((heads, width, width), jnp.float32)

    def local_terms(a_rows, b_rows, c_rows, d_rows, e_rows):
        return segment_terms(a_rows, b_rows, c_rows, d_rows, e_rows, starts)

    terms, terms_back = jax.vjp(local_terms, query_f, key_f, value_f, logits, log_gate)
    linear, offset = segment_map(terms, zero_state)
    local_back = jax.vjp(output_from_terms, terms, zero_state)[1]((cotangent, zero_state))[1]
    owned = to_owners(jnp.stack([linear, offset, local_back], axis=1))
    owned = jnp.stack(chains(owned[:, 0], owned[:, 1], owned[:, 2]), axis=1)
    owned = to_owners(owned)
    state_in, end_grad = owned[:, 0], owned[:, 1]
    unused, full_pull = jax.vjp(output_from_terms, terms, state_in)
    term_grads = full_pull((cotangent, end_grad))[0]
    grads = terms_back(term_grads)
    logit_grad = grads[3]
    piece = hidden_in.astype(jnp.float32)
    partial = jnp.dot(piece.T, logit_grad, precision=highest, preferred_element_type=jnp.float32)
    parts = lax.axis_size("dp") * ctx_count
    partial = partial.reshape(parts, partial.shape[0] // parts, heads)
    beta_weight_grad = jnp.sum(
        lax.all_to_all(partial, ("dp", "ctx"), 0, 0, tiled=True), axis=0
    )
    return (
        grads[0].astype(jnp.bfloat16),
        grads[1].astype(jnp.bfloat16),
        grads[2].astype(jnp.bfloat16),
        grads[4],
        beta_weight_grad,
    )


def solution(mesh):
    in_specs = (
        P(("dp", "ctx"), None),
        P(("dp", "ctx"), None),
        P(("dp", "ctx"), None),
        P(("dp", "ctx"), None),
        P(),
        P(None, ("dp", "ctx")),
        P(("dp", "ctx"), None),
        P("dp", None),
        P(),
        P(),
    )
    out_specs = (
        P(("dp", "ctx"), None),
        P(("dp", "ctx"), None),
        P(("dp", "ctx"), None),
        P(None, ("dp", "ctx")),
        P(("dp", "ctx"), None),
    )
    return jax.shard_map(local, mesh=mesh, in_specs=in_specs, out_specs=out_specs, check_vma=False)
```

```python
import jax
import jax.numpy as jnp
from jax import lax
from jax.experimental import pallas as pl
from jax.experimental.pallas import tpu as pltpu
from jax.sharding import PartitionSpec as P

F32 = jnp.float32
BF16 = jnp.bfloat16
N = 128
HP = 4
VMEM_LIMIT = 56 * 1024 * 1024
NN = (((1,), (0,)), ((), ()))
NT = (((1,), (1,)), ((), ()))
TN = (((0,), (0,)), ((), ()))


def split(x):
    hi = x.astype(BF16)
    return hi, (x - hi.astype(F32)).astype(BF16)


def dot(a, b, dims):
    return lax.dot_general(a, b, dims, preferred_element_type=F32)


def dot3(a, b, dims):
    ah, al = split(a)
    bh, bl = split(b)
    return dot(ah, bh, dims) + (dot(ah, bl, dims) + dot(al, bh, dims))


def dot2l(a, b, dims):
    ah, al = split(a)
    return dot(ah, b, dims) + dot(al, b, dims)


def dot2r(a, b, dims):
    bh, bl = split(b)
    return dot(a, bh, dims) + dot(a, bl, dims)


def iota(axis):
    return lax.broadcasted_iota(jnp.int32, (N, N), axis)


def unit_inverse(lower):
    rows, cols = iota(0), iota(1)
    size = 2
    inverse = jnp.where(rows == cols, 1.0, 0.0) - jnp.where(rows // 2 == cols // 2, lower, 0.0)
    while size < N:
        off = (rows // (2 * size) == cols // (2 * size)) & (rows // size != cols // size)
        step = dot3(jnp.where(off, lower, 0.0), inverse, NN)
        inverse = inverse - dot3(inverse, step, NN)
        size *= 2
    return inverse


def begins_of(lens_ref):
    begins, at = [], jnp.int32(0)
    for i in range(lens_ref.shape[1]):
        begins.append(at)
        at = at + lens_ref[0, i]
    return begins


def plan(lens_ref, ctx):
    begins = begins_of(lens_ref)
    first = ctx * N
    row_pos, col_pos = iota(0) + first, iota(1) + first

    def count(at):
        return sum((b <= at).astype(jnp.int32) for b in begins)

    row_id, col_id = count(row_pos), count(col_pos)
    linked = jnp.where((row_id == col_id) & (row_pos >= col_pos), 1.0, 0.0)
    head = jnp.where(row_id == count(first - 1), 1.0, 0.0)
    tail = jnp.where(row_id == count(first + N - 1), 1.0, 0.0)
    return linked, head, tail, row_id


def token_weights(lens_ref, prompts_ref, rewards_row, prompts_row, row_id, dp):
    rolls = lens_ref.shape[1]
    lanes = lax.broadcasted_iota(jnp.int32, rewards_row.shape, 1)
    weight = jnp.zeros((N, N), F32)
    for i in range(rolls):
        at = dp * rolls + i
        same = jnp.where(prompts_row == prompts_ref[0, at], 1.0, 0.0)
        mean = jnp.sum(same * rewards_row, axis=1, keepdims=True) / jnp.sum(same, axis=1, keepdims=True)
        own = jnp.sum(jnp.where(lanes == at, rewards_row, 0.0), axis=1, keepdims=True)
        length = jnp.full((1, 1), lens_ref[0, i], jnp.int32).astype(F32)
        scale = (own - mean) * (16.0 * N) / (rolls * length)
        weight = jnp.where(row_id == i + 1, scale, weight)
    return weight


def inverse_norm(rows):
    total = jnp.sum(rows * rows, axis=1, keepdims=True)
    return jnp.broadcast_to(lax.rsqrt(total + 1e-06), (N, N))


def by_row(row):
    return jnp.broadcast_to(row, (N, N)).T


def head_terms(q, k, gate_row, beta_row, linked, head, tail):
    qf, kf = q.astype(F32), k.astype(F32)
    rq, rk = inverse_norm(qf), inverse_norm(kf)
    rk_cols = rk.T
    gate = by_row(gate_row)
    decay = jnp.exp(jnp.minimum(gate - gate_row, 0.0)) * linked
    pairs = dot(jnp.concatenate([k, q], axis=0), k, NT)
    key_key = pairs[:N] * rk * rk_cols
    query_key = pairs[N:] * rq * rk_cols
    from_head = head * jnp.exp(gate)
    to_tail = tail * jnp.exp(gate[N - 1 : N, :] - gate)
    return qf * rq, kf * rk, rq, rk, rk_cols, decay, key_key, query_key, from_head, to_tail, by_row(beta_row)


def maps_kernel(lens_ref, prompts_ref, rewards_row_ref, prompts_row_ref, gate_ref, weight_ref, hidden_ref,
                q_ref, k_ref, v_ref, g_ref,
                maps_ref, inv_ref, mg_ref, sum_ref, beta_ref, tw_ref,
                linked_s, head_s, tail_s):
    ctx, dp = lax.axis_index("ctx"), lax.axis_index("dp")

    @pl.when(pl.program_id(0) == 0)
    def _():
        linked, head, tail, row_id = plan(lens_ref, ctx)
        linked_s[...], head_s[...], tail_s[...] = linked, head, tail
        tw_ref[...] = token_weights(lens_ref, prompts_ref, rewards_row_ref[...], prompts_row_ref[...], row_id, dp)
        logits = dot(weight_ref[...], hidden_ref[...], NT)
        beta_ref[...] = 1.0 / (1.0 + jnp.exp(-logits))
        upto = jnp.where(iota(0) <= iota(1), 1.0, 0.0).astype(BF16)
        gates = gate_ref[...]
        hi, rest = split(gates)
        mid = gates - hi.astype(F32)
        mid, low = split(mid)
        sum_ref[...] = dot(hi, upto, NN) + (dot(mid, upto, NN) + dot(low, upto, NN))

    linked, head, tail, tw = linked_s[...], head_s[...], tail_s[...], tw_ref[...]
    strict = iota(0) > iota(1)
    for i in range(HP):
        h = pl.program_id(0) * HP + i
        cols = slice(i * N, (i + 1) * N)
        q, k, v, g = q_ref[:, cols], k_ref[:, cols], v_ref[:, cols], g_ref[:, cols]
        gate_row, beta_row = sum_ref[pl.ds(h, 1), :], beta_ref[pl.ds(h, 1), :]
        qn, kn, rq, rk, rk_cols, decay, key_key, query_key, from_head, to_tail, beta = head_terms(
            q, k, gate_row, beta_row, linked, head, tail)
        inverse = unit_inverse(jnp.where(strict, beta * decay * key_key, 0.0))
        inv_ref[i] = inverse
        mixing = decay * query_key
        sides = jnp.concatenate([beta * v.astype(F32), beta * from_head * kn], axis=1)
        uz = dot3(inverse, sides, NN)
        ends = dot3(uz, to_tail * kn, TN)
        mg = dot2l(mixing * tw, g, TN)
        mg_ref[i] = mg
        back = dot2r(g, tw * from_head * qn, TN) - dot3(mg, uz[:, N:], TN)
        same = jnp.where(iota(0) == iota(1), 1.0, 0.0)
        maps_ref[i, 0] = from_head[N - 1 : N, :] * same - ends[N:]
        maps_ref[i, 1] = ends[:N]
        maps_ref[i, 2] = back


def chains_kernel(maps_ref, out_ref):
    count = maps_ref.shape[0]
    state = jnp.zeros((N, N), F32)
    grad = jnp.zeros((N, N), F32)
    for j in range(count):
        b = count - 1 - j
        out_ref[j, 0] = state
        out_ref[b, 1] = grad
        if j < count - 1:
            state = dot3(state, maps_ref[j, 0], NN) + maps_ref[j, 1]
            grad = dot3(grad, maps_ref[b, 0], NT) + maps_ref[b, 2]


def grads_kernel(lens_ref, q_ref, k_ref, v_ref, g_ref, ends_ref, inv_ref, mg_ref, sum_ref, beta_ref, tw_ref, spread_ref,
                 dq_ref, dk_ref, dv_ref, dgate_ref, dw_ref,
                 linked_s, head_s, tail_s, dlogit_s):
    ctx = lax.axis_index("ctx")

    @pl.when(pl.program_id(0) == 0)
    def _():
        linked_s[...], head_s[...], tail_s[...], unused = plan(lens_ref, ctx)
        dlogit_s[...] = jnp.zeros((N, N), F32)

    linked, head, tail, tw = linked_s[...], head_s[...], tail_s[...], tw_ref[...]
    strict = iota(0) > iota(1)
    reach = iota(0) >= iota(1)
    last = jnp.where(lax.broadcasted_iota(jnp.int32, (N, 1), 0) == N - 1, 1.0, 0.0)
    for i in range(HP):
        h = pl.program_id(0) * HP + i
        cols = slice(i * N, (i + 1) * N)
        q, k, v, g = q_ref[:, cols], k_ref[:, cols], v_ref[:, cols], g_ref[:, cols]
        gate_row, beta_row = sum_ref[pl.ds(h, 1), :], beta_ref[pl.ds(h, 1), :]
        qn, kn, rq, rk, rk_cols, decay, key_key, query_key, from_head, to_tail, beta = head_terms(
            q, k, gate_row, beta_row, linked, head, tail)
        state, grad = ends_ref[i, 0], ends_ref[i, 1]
        inverse = inv_ref[i]
        key_ends = dot2r(k, jnp.concatenate([state, grad], axis=0), NT)
        inner = v.astype(F32) - from_head * rk * key_ends[:, :N]
        u = dot3(inverse, beta * inner, NN)
        du = mg_ref[i] + to_tail * rk * key_ends[:, N:]
        dx = dot3(inverse, du, TN)
        dinv = jnp.where(strict, -dot3(dx, u, NT), 0.0)
        dmix = tw * dot2r(g, u, NT)
        dtail = dot3(u, grad, NN)
        gs = tw * dot2r(g, state, NN)
        dxs = dot3(dx, state, NN)
        decay_dinv = decay * dinv
        pair = beta * decay_dinv
        dqk = decay * dmix
        both = dot2l(jnp.concatenate([dqk * rk_cols, (pair + pair.T) * rk_cols], axis=0), k, NN)
        dqn = from_head * gs + both[:N]
        dkn = dot2l(dqk * rq, q, TN) + to_tail * dtail - beta * from_head * dxs + both[N:]
        dq_ref[:, cols] = (rq * (dqn - qn * jnp.sum(dqn * qn, axis=1, keepdims=True))).astype(BF16)
        dk_ref[:, cols] = (rk * (dkn - kn * jnp.sum(dkn * kn, axis=1, keepdims=True))).astype(BF16)
        dv_ref[:, cols] = (beta * dx).astype(BF16)
        dbeta = jnp.sum(dx * inner + decay_dinv * key_key, axis=1, keepdims=True)
        dlogit_s[...] = jnp.where(iota(1) == h, dbeta * beta * (1.0 - beta), dlogit_s[...])
        spread = dqk * query_key + pair * key_key
        tails = jnp.sum(to_tail * dtail * kn, axis=1, keepdims=True)
        heads = jnp.sum(from_head * (gs * qn - beta * dxs * kn), axis=1, keepdims=True)
        through = jnp.sum(from_head[N - 1 : N, :] * jnp.sum(state * grad, axis=0, keepdims=True), axis=1, keepdims=True)
        dgamma = jnp.sum(spread, axis=1, keepdims=True) + heads - tails
        dgamma = dgamma + last * (jnp.sum(tails, axis=0, keepdims=True) + through)
        dgamma = dgamma - by_row(jnp.sum(spread, axis=0, keepdims=True))
        dgate_ref[pl.ds(h, 1), :] = jnp.sum(jnp.where(reach, dgamma, 0.0), axis=0, keepdims=True)

    @pl.when(pl.program_id(0) == pl.num_programs(0) - 1)
    def _():
        heads = beta_ref.shape[0]
        per = N // heads
        dlogit = dlogit_s[...]
        rows = spread_ref.shape[0]
        for first in range(0, rows, per):
            total = jnp.zeros((N, N), F32)
            for r in range(first, min(first + per, rows)):
                moved = dlogit if r == first else pltpu.roll(dlogit, heads * (r - first), 1)
                total = total + dot2r(spread_ref[r], moved, NN)
            dw_ref[:, first * heads : first * heads + N] = total


def sum_kernel(parts_ref, out_ref):
    rows, heads = out_ref.shape
    total = jnp.sum(parts_ref[...], axis=0, keepdims=True)
    for r in range(rows):
        out_ref[r : r + 1, :] = total[:, r * heads : (r + 1) * heads]


def whole(shape):
    return pl.BlockSpec(shape, lambda i: (0,) * len(shape))


def to_owners(x):
    return lax.all_to_all(x, "ctx", 0, 0, tiled=True)


def local(queries, key_rows, value_rows, hidden_in, beta_weight, log_gate, out_grad, lengths, rewards, prompts):
    tokens, width = queries.shape
    depth, heads = beta_weight.shape
    parts = lax.axis_size("dp") * lax.axis_size("ctx")
    owned_rows = depth // parts
    tiles = -(-owned_rows * heads // N)
    smem = pl.BlockSpec(memory_space=pltpu.SMEM)
    by_heads = pl.BlockSpec((tokens, HP * N), lambda i: (0, i))
    params = pltpu.CompilerParams(vmem_limit_bytes=VMEM_LIMIT)
    prompts_row, rewards_row = prompts.reshape(1, -1), rewards.reshape(1, -1)

    def square(n):
        return pl.BlockSpec((HP, n, N, N), lambda i: (i, 0, 0, 0))

    one_square = pl.BlockSpec((HP, N, N), lambda i: (i, 0, 0))
    masks = [pltpu.VMEM((N, N), F32)] * 3
    maps, inverse, mg, sums, beta, tw = pl.pallas_call(
        maps_kernel,
        grid=(heads // HP,),
        in_specs=[smem, smem, whole(rewards_row.shape), whole(prompts_row.shape), whole(log_gate.shape),
                  whole((heads, depth)), whole(hidden_in.shape)] + [by_heads] * 4,
        out_specs=[square(3), one_square, one_square, whole((heads, N)), whole((heads, N)), whole((N, N))],
        out_shape=[jax.ShapeDtypeStruct(s, F32) for s in (
            (heads, 3, N, N), (heads, N, N), (heads, N, N), (heads, N), (heads, N), (N, N))],
        scratch_shapes=masks,
        compiler_params=params,
        name="segment_maps",
    )(lengths, prompts_row, rewards_row, prompts_row, log_gate, beta_weight.T, hidden_in,
      queries, key_rows, value_rows, out_grad)
    owned = to_owners(maps)
    ends = pl.pallas_call(
        chains_kernel,
        out_shape=jax.ShapeDtypeStruct((owned.shape[0], 2, N, N), F32),
        in_specs=[pl.BlockSpec(memory_space=pltpu.VMEM)],
        out_specs=pl.BlockSpec(memory_space=pltpu.VMEM),
        compiler_params=params,
        name="chains",
    )(owned)
    ends = to_owners(ends)
    spread = hidden_in.T.reshape(parts, owned_rows, tokens).transpose(1, 0, 2)
    dq, dk, dv, dgate, dw = pl.pallas_call(
        grads_kernel,
        grid=(heads // HP,),
        in_specs=[smem] + [by_heads] * 4 + [square(2), one_square, one_square, whole((heads, N)), whole((heads, N)),
                                            whole((N, N)), whole(spread.shape)],
        out_specs=[by_heads] * 3 + [whole((heads, N)), whole((parts, tiles * N))],
        out_shape=[jax.ShapeDtypeStruct((tokens, width), BF16)] * 3
        + [jax.ShapeDtypeStruct((heads, N), F32), jax.ShapeDtypeStruct((parts, tiles * N), F32)],
        scratch_shapes=masks + [pltpu.VMEM((N, N), F32)],
        compiler_params=params,
        name="segment_grads",
    )(lengths, queries, key_rows, value_rows, out_grad, ends, inverse, mg, sums, beta, tw, spread)
    pieces = lax.all_to_all(dw, ("dp", "ctx"), 0, 0, tiled=True)
    dweight = pl.pallas_call(
        sum_kernel,
        out_shape=jax.ShapeDtypeStruct((owned_rows, heads), F32),
        in_specs=[pl.BlockSpec(memory_space=pltpu.VMEM)],
        out_specs=pl.BlockSpec(memory_space=pltpu.VMEM),
        name="sum_parts",
    )(pieces)
    return dq, dk, dv, dgate, dweight


def solution(mesh):
    rows = P(("dp", "ctx"), None)
    gates = P(None, ("dp", "ctx"))
    in_specs = (rows, rows, rows, rows, P(), gates, rows, P("dp", None), P(), P())
    out_specs = (rows, rows, rows, gates, rows)
    return jax.shard_map(local, mesh=mesh, in_specs=in_specs, out_specs=out_specs, check_vma=False)
```

```python
import jax
import jax.numpy as jnp
from jax import lax
from jax.experimental import pallas as pl
from jax.experimental.pallas import tpu as pltpu
from jax.sharding import PartitionSpec as P

F32 = jnp.float32
BF16 = jnp.bfloat16
N = 128
HP = 8
HG = 4
VMEM_LIMIT = 56 * 1024 * 1024
NN = (((1,), (0,)), ((), ()))
NT = (((1,), (1,)), ((), ()))
TN = (((0,), (0,)), ((), ()))


def split(x):
    hi = x.astype(BF16)
    return hi, (x - hi.astype(F32)).astype(BF16)


def dot(a, b, dims):
    return lax.dot_general(a, b, dims, preferred_element_type=F32)


def dot3(a, b, dims):
    (ka,), (kb,) = dims[0]
    n = b.shape[1 - kb]
    rights = jnp.concatenate(split(b), 1 - kb)
    both = dot(jnp.concatenate(split(a), ka), jnp.concatenate([rights, rights], kb), dims)
    return both[:, :n] + both[:, n:]


def dot2l(a, b, dims):
    (ka,), (kb,) = dims[0]
    return dot(jnp.concatenate(split(a), ka), jnp.concatenate([b, b], kb), dims)


def dot2r(a, b, dims):
    (ka,), (kb,) = dims[0]
    return dot(jnp.concatenate([a, a], ka), jnp.concatenate(split(b), kb), dims)


def iota(axis):
    return lax.broadcasted_iota(jnp.int32, (N, N), axis)


def unit_inverses(lowers):
    rows, cols = iota(0), iota(1)
    same = jnp.where(rows == cols, 1.0, 0.0)
    pair = jnp.where(rows // 2 == cols // 2, 1.0, 0.0)
    inverses = [same - pair * lower for lower in lowers]
    size = 2
    while size < N:
        off = jnp.where((rows // (2 * size) == cols // (2 * size)) & (rows // size != cols // size), 1.0, 0.0)
        steps = [dot3(off * lower, inverse, NN) for lower, inverse in zip(lowers, inverses)]
        inverses = [inverse - dot3(inverse, step, NN) for inverse, step in zip(inverses, steps)]
        size *= 2
    return inverses


def begins_of(lens_ref):
    begins, at = [], jnp.int32(0)
    for i in range(lens_ref.shape[1]):
        begins.append(at)
        at = at + lens_ref[0, i]
    return begins


def plan(lens_ref, ctx):
    begins = begins_of(lens_ref)
    first = ctx * N
    row_pos, col_pos = iota(0) + first, iota(1) + first

    def count(at):
        return sum((b <= at).astype(jnp.int32) for b in begins)

    row_id, col_id = count(row_pos), count(col_pos)
    linked = jnp.where((row_id == col_id) & (row_pos >= col_pos), 1.0, 0.0)
    head = jnp.where(row_id == count(first - 1), 1.0, 0.0)
    tail = jnp.where(row_id == count(first + N - 1), 1.0, 0.0)
    return linked, head, tail, row_id


def token_weights(lens_ref, prompts_ref, rewards_row, prompts_row, row_id, dp):
    rolls = lens_ref.shape[1]
    lanes = lax.broadcasted_iota(jnp.int32, rewards_row.shape, 1)
    weight = jnp.zeros((N, N), F32)
    for i in range(rolls):
        at = dp * rolls + i
        same = jnp.where(prompts_row == prompts_ref[0, at], 1.0, 0.0)
        mean = jnp.sum(same * rewards_row, axis=1, keepdims=True) / jnp.sum(same, axis=1, keepdims=True)
        own = jnp.sum(jnp.where(lanes == at, rewards_row, 0.0), axis=1, keepdims=True)
        length = jnp.full((1, 1), lens_ref[0, i], jnp.int32).astype(F32)
        scale = (own - mean) * (16.0 * N) / (rolls * length)
        weight = jnp.where(row_id == i + 1, scale, weight)
    return weight


def inverse_norm(rows):
    total = jnp.sum(rows * rows, axis=1, keepdims=True)
    return jnp.broadcast_to(lax.rsqrt(total + 1e-06), (N, N))


def by_row(row):
    return jnp.broadcast_to(row, (N, N)).T


def head_terms(q, k, gate_row, beta_row, linked, head, tail):
    qf, kf = q.astype(F32), k.astype(F32)
    rq, rk = inverse_norm(qf), inverse_norm(kf)
    rk_cols = rk.T
    gate = by_row(gate_row)
    decay = jnp.exp(jnp.minimum(gate - gate_row, 0.0)) * linked
    pairs = dot(jnp.concatenate([k, q], axis=0), k, NT)
    key_key = pairs[:N] * rk * rk_cols
    query_key = pairs[N:] * rq * rk_cols
    from_head = head * jnp.exp(gate)
    to_tail = tail * jnp.exp(gate[N - 1 : N, :] - gate)
    return qf * rq, kf * rk, rq, rk, rk_cols, decay, key_key, query_key, from_head, to_tail, by_row(beta_row)


def maps_kernel(lens_ref, prompts_ref, rewards_row_ref, prompts_row_ref, gate_ref, weight_ref, hidden_ref,
                q_ref, k_ref, v_ref, g_ref,
                maps_ref, inv_ref, mg_ref, sum_ref, beta_ref, tw_ref,
                linked_s, head_s, tail_s):
    ctx, dp = lax.axis_index("ctx"), lax.axis_index("dp")

    @pl.when(pl.program_id(0) == 0)
    def _():
        linked, head, tail, row_id = plan(lens_ref, ctx)
        linked_s[...], head_s[...], tail_s[...] = linked, head, tail
        tw_ref[...] = token_weights(lens_ref, prompts_ref, rewards_row_ref[...], prompts_row_ref[...], row_id, dp)
        logits = dot(weight_ref[...], hidden_ref[...], NT)
        beta_ref[...] = 1.0 / (1.0 + jnp.exp(-logits))
        upto = jnp.where(iota(0) <= iota(1), 1.0, 0.0).astype(BF16)
        gates = gate_ref[...]
        hi, rest = split(gates)
        mid = gates - hi.astype(F32)
        mid, low = split(mid)
        sum_ref[...] = dot(hi, upto, NN) + (dot(mid, upto, NN) + dot(low, upto, NN))

    linked, head, tail, tw = linked_s[...], head_s[...], tail_s[...], tw_ref[...]
    strict = jnp.where(iota(0) > iota(1), 1.0, 0.0)
    same = jnp.where(iota(0) == iota(1), 1.0, 0.0)
    lowers, rest = [], []
    for i in range(HP):
        h = pl.program_id(0) * HP + i
        cols = slice(i * N, (i + 1) * N)
        q, k, v, g = q_ref[:, cols], k_ref[:, cols], v_ref[:, cols], g_ref[:, cols]
        gate_row, beta_row = sum_ref[pl.ds(h, 1), :], beta_ref[pl.ds(h, 1), :]
        qn, kn, rq, rk, rk_cols, decay, key_key, query_key, from_head, to_tail, beta = head_terms(
            q, k, gate_row, beta_row, linked, head, tail)
        lowers.append(strict * (beta * decay * key_key))
        mg_ref[i] = dot2l(decay * query_key * tw, g, TN)
        maps_ref[i, 2] = dot2r(g, tw * from_head * qn, TN)
        maps_ref[i, 0] = from_head[N - 1 : N, :] * same
        rest.append((jnp.concatenate([beta * v.astype(F32), beta * from_head * kn], axis=1), to_tail * kn))
    inverses = unit_inverses(lowers)
    for i in range(HP):
        inv_ref[i] = inverses[i]
    uzs = [dot3(inverse, sides, NN) for inverse, (sides, _) in zip(inverses, rest)]
    for i in range(HP):
        ends = dot3(uzs[i], rest[i][1], TN)
        maps_ref[i, 0] -= ends[N:]
        maps_ref[i, 1] = ends[:N]
        maps_ref[i, 2] -= dot3(mg_ref[i], uzs[i][:, N:], TN)


def chains_kernel(maps_ref, out_ref):
    count = maps_ref.shape[0]
    state = jnp.zeros((N, N), F32)
    grad = jnp.zeros((N, N), F32)
    for j in range(count):
        b = count - 1 - j
        out_ref[j, 0] = state
        out_ref[b, 1] = grad
        if j < count - 1:
            state = dot3(state, maps_ref[j, 0], NN) + maps_ref[j, 1]
            grad = dot3(grad, maps_ref[b, 0], NT) + maps_ref[b, 2]


def logits_kernel(lens_ref, q_ref, k_ref, v_ref, ends_ref, inv_ref, mg_ref, sum_ref, beta_ref, spread_ref,
                  u_ref, dx_ref, dw_ref,
                  linked_s, head_s, tail_s, dlogit_s):
    ctx = lax.axis_index("ctx")

    @pl.when(pl.program_id(0) == 0)
    def _():
        linked_s[...], head_s[...], tail_s[...], unused = plan(lens_ref, ctx)
        dlogit_s[...] = jnp.zeros((N, N), F32)

    linked, head, tail = linked_s[...], head_s[...], tail_s[...]
    strict = jnp.where(iota(0) > iota(1), 1.0, 0.0)
    heads = range(HP)
    first, inners, betas, pairs, dus, us, dxs = pl.program_id(0) * HP, [], [], [], [], [], []
    for i in heads:
        cols = slice(i * N, (i + 1) * N)
        q, k, v = q_ref[:, cols], k_ref[:, cols], v_ref[:, cols]
        gate_row, beta_row = sum_ref[pl.ds(first + i, 1), :], beta_ref[pl.ds(first + i, 1), :]
        kf = k.astype(F32)
        rk = inverse_norm(kf)
        gate = by_row(gate_row)
        key_key = dot(k, k, NT) * rk * rk.T
        pairs.append(strict * linked * jnp.exp(jnp.minimum(gate - gate_row, 0.0)) * key_key)
        key_ends = dot2r(k, jnp.concatenate([ends_ref[i, 0], ends_ref[i, 1]], axis=0), NT)
        inners.append(v.astype(F32) - head * jnp.exp(gate) * rk * key_ends[:, :N])
        dus.append(mg_ref[i] + tail * jnp.exp(gate[N - 1 : N, :] - gate) * rk * key_ends[:, N:])
        betas.append(by_row(beta_row))
    for i in heads:
        us.append(dot3(inv_ref[i], betas[i] * inners[i], NN))
        dxs.append(dot3(inv_ref[i], dus[i], TN))
    for i in heads:
        u_ref[i], dx_ref[i] = us[i], dxs[i]
    dlogit = dlogit_s[...]
    for i in heads:
        dbeta = jnp.sum(dxs[i] * inners[i] - dot3(dxs[i], us[i], NT) * pairs[i], axis=1, keepdims=True)
        dlogit = jnp.where(iota(1) == first + i, dbeta * betas[i] * (1.0 - betas[i]), dlogit)
    dlogit_s[...] = dlogit

    @pl.when(pl.program_id(0) == pl.num_programs(0) - 1)
    def _():
        count = beta_ref.shape[0]
        per = N // count
        rows = spread_ref.shape[0]
        for first in range(0, rows, per):
            total = jnp.zeros((N, N), F32)
            for r in range(first, min(first + per, rows)):
                moved = dlogit if r == first else pltpu.roll(dlogit, count * (r - first), 1)
                total = total + dot2r(spread_ref[r], moved, NN)
            dw_ref[:, 0, first * count : first * count + N] = total


def grads_kernel(lens_ref, q_ref, k_ref, g_ref, ends_ref, u_ref, dx_ref, sum_ref, beta_ref, tw_ref,
                 dq_ref, dk_ref, dv_ref, dgate_ref,
                 linked_s, head_s, tail_s):
    ctx = lax.axis_index("ctx")

    @pl.when(pl.program_id(0) == 0)
    def _():
        linked_s[...], head_s[...], tail_s[...], unused = plan(lens_ref, ctx)

    linked, head, tail, tw = linked_s[...], head_s[...], tail_s[...], tw_ref[...]
    strict = jnp.where(iota(0) > iota(1), 1.0, 0.0)
    reach = iota(0) >= iota(1)
    last = jnp.where(lax.broadcasted_iota(jnp.int32, (N, 1), 0) == N - 1, 1.0, 0.0)
    for i in range(HG):
        h = pl.program_id(0) * HG + i
        cols = slice(i * N, (i + 1) * N)
        q, k, g = q_ref[:, cols], k_ref[:, cols], g_ref[:, cols]
        gate_row, beta_row = sum_ref[pl.ds(h, 1), :], beta_ref[pl.ds(h, 1), :]
        qn, kn, rq, rk, rk_cols, decay, key_key, query_key, from_head, to_tail, beta = head_terms(
            q, k, gate_row, beta_row, linked, head, tail)
        state, grad, u, dx = ends_ref[i, 0], ends_ref[i, 1], u_ref[i], dx_ref[i]
        pair = -(strict * beta * decay) * dot3(dx, u, NT)
        dqk = decay * (tw * dot2r(g, u, NT))
        dtail = dot3(u, grad, NN)
        gs = tw * dot2r(g, state, NN)
        dxs = dot3(dx, state, NN)
        both = dot2l(jnp.concatenate([dqk * rk_cols, (pair + pair.T) * rk_cols], axis=0), k, NN)
        dqn = from_head * gs + both[:N]
        dkn = dot2l(dqk * rq, q, TN) + to_tail * dtail - beta * from_head * dxs + both[N:]
        dq_ref[:, cols] = (rq * (dqn - qn * jnp.sum(dqn * qn, axis=1, keepdims=True))).astype(BF16)
        dk_ref[:, cols] = (rk * (dkn - kn * jnp.sum(dkn * kn, axis=1, keepdims=True))).astype(BF16)
        dv_ref[:, cols] = (beta * dx).astype(BF16)
        spread = dqk * query_key + pair * key_key
        tails = jnp.sum(to_tail * dtail * kn, axis=1, keepdims=True)
        heads = jnp.sum(from_head * (gs * qn - beta * dxs * kn), axis=1, keepdims=True)
        through = jnp.sum(from_head[N - 1 : N, :] * jnp.sum(state * grad, axis=0, keepdims=True), axis=1, keepdims=True)
        dgamma = jnp.sum(spread, axis=1, keepdims=True) + heads - tails
        dgamma = dgamma + last * (jnp.sum(tails, axis=0, keepdims=True) + through)
        dgamma = dgamma - by_row(jnp.sum(spread, axis=0, keepdims=True))
        dgate_ref[pl.ds(h, 1), :] = jnp.sum(jnp.where(reach, dgamma, 0.0), axis=0, keepdims=True)


def sum_kernel(parts_ref, out_ref, rows_s):
    heads, rows = out_ref.shape
    total = jnp.sum(parts_ref[:, 0, :], axis=0, keepdims=True)
    rows_s[...] = jnp.zeros((N, N), F32)
    for r in range(rows):
        rows_s[r : r + 1, :heads] = total[:, r * heads : (r + 1) * heads]
    out_ref[...] = rows_s[...].T[:heads, :rows]


def whole(shape):
    return pl.BlockSpec(shape, lambda i: (0,) * len(shape))


def to_owners(x):
    return lax.all_to_all(x, "ctx", 0, 0, tiled=True)


def local(queries, key_rows, value_rows, hidden_in, beta_weight, log_gate, out_grad, lengths, rewards, prompts):
    tokens, width = queries.shape
    depth, heads = beta_weight.shape
    parts = lax.axis_size("dp") * lax.axis_size("ctx")
    owned_rows = depth // parts
    tiles = -(-owned_rows * heads // N)
    smem = pl.BlockSpec(memory_space=pltpu.SMEM)
    by_heads = pl.BlockSpec((tokens, HP * N), lambda i: (0, i))
    params = pltpu.CompilerParams(vmem_limit_bytes=VMEM_LIMIT)
    prompts_row, rewards_row = prompts.reshape(1, -1), rewards.reshape(1, -1)

    def square(n):
        return pl.BlockSpec((HP, n, N, N), lambda i: (i, 0, 0, 0))

    one_square = pl.BlockSpec((HP, N, N), lambda i: (i, 0, 0))
    masks = [pltpu.VMEM((N, N), F32)] * 3
    maps, inverse, mg, sums, beta, tw = pl.pallas_call(
        maps_kernel,
        grid=(heads // HP,),
        in_specs=[smem, smem, whole(rewards_row.shape), whole(prompts_row.shape), whole(log_gate.shape),
                  whole((heads, depth)), whole(hidden_in.shape)] + [by_heads] * 4,
        out_specs=[square(3), one_square, one_square, whole((heads, N)), whole((heads, N)), whole((N, N))],
        out_shape=[jax.ShapeDtypeStruct(s, F32) for s in (
            (heads, 3, N, N), (heads, N, N), (heads, N, N), (heads, N), (heads, N), (N, N))],
        scratch_shapes=masks,
        compiler_params=params,
        name="segment_maps",
    )(lengths, prompts_row, rewards_row, prompts_row, log_gate, beta_weight.T, hidden_in,
      queries, key_rows, value_rows, out_grad)
    owned = to_owners(maps)
    ends = pl.pallas_call(
        chains_kernel,
        out_shape=jax.ShapeDtypeStruct((owned.shape[0], 2, N, N), F32),
        in_specs=[pl.BlockSpec(memory_space=pltpu.VMEM)],
        out_specs=pl.BlockSpec(memory_space=pltpu.VMEM),
        compiler_params=params,
        name="chains",
    )(owned)
    ends = to_owners(ends)
    spread = hidden_in.T.reshape(parts, owned_rows, tokens).transpose(1, 0, 2)
    u, dx, dw = pl.pallas_call(
        logits_kernel,
        grid=(heads // HP,),
        in_specs=[smem] + [by_heads] * 3 + [square(2), one_square, one_square, whole((heads, N)), whole((heads, N)),
                                            whole(spread.shape)],
        out_specs=[one_square] * 2 + [whole((parts, 1, tiles * N))],
        out_shape=[jax.ShapeDtypeStruct((heads, N, N), F32)] * 2
        + [jax.ShapeDtypeStruct((parts, 1, tiles * N), F32)],
        scratch_shapes=masks + [pltpu.VMEM((N, N), F32)],
        compiler_params=params,
        name="logit_grads",
    )(lengths, queries, key_rows, value_rows, ends, inverse, mg, sums, beta, spread)
    pieces = lax.all_to_all(dw, ("dp", "ctx"), 0, 0, tiled=True)
    few_heads = pl.BlockSpec((tokens, HG * N), lambda i: (0, i))
    few_squares = pl.BlockSpec((HG, N, N), lambda i: (i, 0, 0))
    dq, dk, dv, dgate = pl.pallas_call(
        grads_kernel,
        grid=(heads // HG,),
        in_specs=[smem] + [few_heads] * 3 + [pl.BlockSpec((HG, 2, N, N), lambda i: (i, 0, 0, 0)), few_squares, few_squares,
                                             whole((heads, N)), whole((heads, N)), whole((N, N))],
        out_specs=[few_heads] * 3 + [whole((heads, N))],
        out_shape=[jax.ShapeDtypeStruct((tokens, width), BF16)] * 3 + [jax.ShapeDtypeStruct((heads, N), F32)],
        scratch_shapes=masks,
        compiler_params=params,
        cost_estimate=pl.CostEstimate(flops=12_000_000_000, bytes_accessed=40_000_000, transcendentals=0),
        name="segment_grads",
    )(lengths, queries, key_rows, out_grad, ends, u, dx, sums, beta, tw)
    dweight = pl.pallas_call(
        sum_kernel,
        out_shape=jax.ShapeDtypeStruct((heads, owned_rows), F32),
        in_specs=[pl.BlockSpec(memory_space=pltpu.VMEM)],
        out_specs=pl.BlockSpec(memory_space=pltpu.VMEM),
        scratch_shapes=[pltpu.VMEM((N, N), F32)],
        name="sum_parts",
    )(pieces)
    return dq, dk, dv, dgate, dweight.T


def solution(mesh):
    rows = P(("dp", "ctx"), None)
    gates = P(None, ("dp", "ctx"))
    in_specs = (rows, rows, rows, rows, P(), gates, rows, P("dp", None), P(), P())
    out_specs = (rows, rows, rows, gates, rows)
    return jax.shard_map(local, mesh=mesh, in_specs=in_specs, out_specs=out_specs, check_vma=False)
```

```python
import jax
import jax.numpy as jnp
from jax import lax
from jax.experimental import pallas as pl
from jax.experimental.pallas import tpu as pltpu
from jax.sharding import PartitionSpec as P

F32 = jnp.float32
BF16 = jnp.bfloat16
N = 128
HP = 8
HG = 4
VMEM_LIMIT = 56 * 1024 * 1024
VMEM_SMALL = 40 * 1024 * 1024
NN = (((1,), (0,)), ((), ()))
NT = (((1,), (1,)), ((), ()))
TN = (((0,), (0,)), ((), ()))


def split(x):
    hi = x.astype(BF16)
    return hi, (x - hi.astype(F32)).astype(BF16)


def dot(a, b, dims):
    return lax.dot_general(a, b, dims, preferred_element_type=F32)


def dot3(a, b, dims):
    return parts_dot(jnp.concatenate(split(a), dims[0][0][0]), b, dims)


def parts_dot(a_parts, b, dims):
    kb = dims[0][1][0]
    n = b.shape[1 - kb]
    rights = jnp.concatenate(split(b), 1 - kb)
    both = dot(a_parts, jnp.concatenate([rights, rights], kb), dims)
    return both[:, :n] + both[:, n:]


def dot2l(a, b, dims):
    (ka,), (kb,) = dims[0]
    return dot(jnp.concatenate(split(a), ka), jnp.concatenate([b, b], kb), dims)


def dot2r(a, b, dims):
    (ka,), (kb,) = dims[0]
    return dot(jnp.concatenate([a, a], ka), jnp.concatenate(split(b), kb), dims)


def iota(axis):
    return lax.broadcasted_iota(jnp.int32, (N, N), axis)


def unit_inverses(lowers):
    rows, cols = iota(0), iota(1)
    same = jnp.where(rows == cols, 1.0, 0.0)
    pair = jnp.where(rows // 2 == cols // 2, 1.0, 0.0)
    inverses = [same - pair * lower for lower in lowers]
    size = 2
    while size < N:
        off = jnp.where((rows // (2 * size) == cols // (2 * size)) & (rows // size != cols // size), 1.0, 0.0)
        steps = [dot3(off * lower, inverse, NN) for lower, inverse in zip(lowers, inverses)]
        inverses = [inverse - dot3(inverse, step, NN) for inverse, step in zip(inverses, steps)]
        size *= 2
    return inverses


def begins_of(lens_ref):
    begins, at = [], jnp.int32(0)
    for i in range(lens_ref.shape[1]):
        begins.append(at)
        at = at + lens_ref[0, i]
    return begins


def plan(lens_ref, ctx):
    begins = begins_of(lens_ref)
    first = ctx * N
    row_pos, col_pos = iota(0) + first, iota(1) + first

    def count(at):
        return sum((b <= at).astype(jnp.int32) for b in begins)

    row_id, col_id = count(row_pos), count(col_pos)
    linked = jnp.where((row_id == col_id) & (row_pos >= col_pos), 1.0, 0.0)
    head = jnp.where(row_id == count(first - 1), 1.0, 0.0)
    tail = jnp.where(row_id == count(first + N - 1), 1.0, 0.0)
    return linked, head, tail, row_id


def token_weights(lens_ref, prompts_ref, rewards_row, prompts_row, row_id, dp):
    rolls = lens_ref.shape[1]
    lanes = lax.broadcasted_iota(jnp.int32, rewards_row.shape, 1)
    weight = jnp.zeros((N, N), F32)
    for i in range(rolls):
        at = dp * rolls + i
        same = jnp.where(prompts_row == prompts_ref[0, at], 1.0, 0.0)
        mean = jnp.sum(same * rewards_row, axis=1, keepdims=True) / jnp.sum(same, axis=1, keepdims=True)
        own = jnp.sum(jnp.where(lanes == at, rewards_row, 0.0), axis=1, keepdims=True)
        length = jnp.full((1, 1), lens_ref[0, i], jnp.int32).astype(F32)
        scale = (own - mean) * (16.0 * N) / (rolls * length)
        weight = jnp.where(row_id == i + 1, scale, weight)
    return weight


def inverse_norm(rows):
    total = jnp.sum(rows * rows, axis=1, keepdims=True)
    return jnp.broadcast_to(lax.rsqrt(total + 1e-06), (N, N))


def by_row(row):
    return jnp.broadcast_to(row, (N, N)).T


def head_terms(q, k, gate_row, beta_row, linked, head, tail):
    qf, kf = q.astype(F32), k.astype(F32)
    rq, rk = inverse_norm(qf), inverse_norm(kf)
    rk_cols = rk.T
    gate = by_row(gate_row)
    decay = jnp.exp(jnp.minimum(gate - gate_row, 0.0)) * linked
    pairs = dot(jnp.concatenate([k, q], axis=0), k, NT)
    key_key = pairs[:N] * rk * rk_cols
    query_key = pairs[N:] * rq * rk_cols
    from_head = head * jnp.exp(gate)
    to_tail = tail * jnp.exp(gate[N - 1 : N, :] - gate)
    return qf * rq, kf * rk, rq, rk, rk_cols, decay, key_key, query_key, from_head, to_tail, by_row(beta_row)


def maps_kernel(lens_ref, prompts_ref, rewards_row_ref, prompts_row_ref, gate_ref, weight_ref, hidden_ref,
                q_ref, k_ref, v_ref, g_ref,
                maps_ref, inv_ref, sum_ref, beta_ref, tw_ref,
                linked_s, head_s, tail_s):
    ctx, dp = lax.axis_index("ctx"), lax.axis_index("dp")

    @pl.when(pl.program_id(0) == 0)
    def _():
        linked, head, tail, row_id = plan(lens_ref, ctx)
        linked_s[...], head_s[...], tail_s[...] = linked, head, tail
        tw_ref[...] = token_weights(lens_ref, prompts_ref, rewards_row_ref[...], prompts_row_ref[...], row_id, dp)
        logits = dot(weight_ref[...], hidden_ref[...], NT)
        beta_ref[...] = 1.0 / (1.0 + jnp.exp(-logits))
        upto = jnp.where(iota(0) <= iota(1), 1.0, 0.0).astype(BF16)
        gates = gate_ref[...]
        hi, rest = split(gates)
        mid = gates - hi.astype(F32)
        mid, low = split(mid)
        sum_ref[...] = dot(hi, upto, NN) + (dot(mid, upto, NN) + dot(low, upto, NN))

    linked, head, tail, tw = linked_s[...], head_s[...], tail_s[...], tw_ref[...]
    strict = jnp.where(iota(0) > iota(1), 1.0, 0.0)
    same = jnp.where(iota(0) == iota(1), 1.0, 0.0)
    lowers, rest, mgs = [], [], []
    for i in range(HP):
        h = pl.program_id(0) * HP + i
        cols = slice(i * N, (i + 1) * N)
        q, k, v, g = q_ref[:, cols], k_ref[:, cols], v_ref[:, cols], g_ref[:, cols]
        gate_row, beta_row = sum_ref[pl.ds(h, 1), :], beta_ref[pl.ds(h, 1), :]
        qn, kn, rq, rk, rk_cols, decay, key_key, query_key, from_head, to_tail, beta = head_terms(
            q, k, gate_row, beta_row, linked, head, tail)
        lowers.append(strict * (beta * decay * key_key))
        mgs.append(dot2l(decay * query_key * tw, g, TN))
        maps_ref[i, 2] = dot2r(g, tw * from_head * qn, TN)
        maps_ref[i, 0] = from_head[N - 1 : N, :] * same
        rest.append((jnp.concatenate([beta * v.astype(F32), beta * from_head * kn], axis=1), to_tail * kn))
    inverses = unit_inverses(lowers)
    for i in range(HP):
        inv_ref[i] = inverses[i]
    uzs = [dot3(inverse, sides, NN) for inverse, (sides, _) in zip(inverses, rest)]
    for i in range(HP):
        ends = dot3(uzs[i], rest[i][1], TN)
        maps_ref[i, 0] -= ends[N:]
        maps_ref[i, 1] = ends[:N]
        maps_ref[i, 2] -= dot3(mgs[i], uzs[i][:, N:], TN)


def chains_kernel(maps_ref, out_ref):
    count = maps_ref.shape[0]
    state = jnp.zeros((N, N), F32)
    grad = jnp.zeros((N, N), F32)
    for j in range(count):
        b = count - 1 - j
        out_ref[j, 0] = state
        out_ref[b, 1] = grad
        if j < count - 1:
            state = dot3(state, maps_ref[j, 0], NN) + maps_ref[j, 1]
            grad = dot3(grad, maps_ref[b, 0], NT) + maps_ref[b, 2]


def ahead_kernel(lens_ref, q_ref, k_ref, v_ref, g_ref, inv_ref, sum_ref, beta_ref, tw_ref,
                 u0_ref, z_ref, dx0_ref, x_ref,
                 linked_s, head_s, tail_s):
    ctx = lax.axis_index("ctx")

    @pl.when(pl.program_id(0) == 0)
    def _():
        linked_s[...], head_s[...], tail_s[...], unused = plan(lens_ref, ctx)

    linked, head, tail, tw = linked_s[...], head_s[...], tail_s[...], tw_ref[...]
    for i in range(HG):
        h = pl.program_id(0) * HG + i
        cols = slice(i * N, (i + 1) * N)
        q, k, v, g = q_ref[:, cols], k_ref[:, cols], v_ref[:, cols], g_ref[:, cols]
        gate_row, beta_row = sum_ref[pl.ds(h, 1), :], beta_ref[pl.ds(h, 1), :]
        qn, kn, rq, rk, rk_cols, decay, key_key, query_key, from_head, to_tail, beta = head_terms(
            q, k, gate_row, beta_row, linked, head, tail)
        uz = dot3(inv_ref[i], jnp.concatenate([beta * v.astype(F32), beta * from_head * kn], axis=1), NN)
        u0_ref[i] = uz[:, :N]
        z_ref[i] = jnp.concatenate(split(uz[:, N:]), axis=1)
        mg = dot2l(decay * query_key * tw, g, TN)
        dxx = dot3(inv_ref[i], jnp.concatenate([mg, to_tail * kn], axis=1), TN)
        dx0_ref[i] = dxx[:, :N]
        x_ref[i] = jnp.concatenate(split(dxx[:, N:]), axis=1)


def logits_kernel(ends_ref, u0_ref, z_ref, dx0_ref, x_ref, beta_ref, spread_ref,
                  u_ref, dx_ref, dw_ref, sums_s):
    @pl.when(pl.program_id(0) == 0)
    def _():
        sums_s[...] = jnp.zeros((N, N), F32)

    sums = sums_s[...]
    for i in range(HP):
        u = u0_ref[i] - parts_dot(z_ref[i], ends_ref[i, 0], NT)
        dx = dx0_ref[i] + parts_dot(x_ref[i], ends_ref[i, 1], NT)
        u_ref[i], dx_ref[i] = u, dx
        sums = jnp.where(iota(1) == pl.program_id(0) * HP + i, jnp.sum(dx * u, axis=1, keepdims=True), sums)
    sums_s[...] = sums

    @pl.when(pl.program_id(0) == pl.num_programs(0) - 1)
    def _():
        count = beta_ref.shape[0]
        dlogit = sums * (1.0 - jnp.concatenate([beta_ref[...], jnp.zeros((N - count, N), F32)], axis=0).T)
        per = N // count
        rows = spread_ref.shape[0]
        for first in range(0, rows, per):
            total = jnp.zeros((N, N), F32)
            for r in range(first, min(first + per, rows)):
                moved = dlogit if r == first else pltpu.roll(dlogit, count * (r - first), 1)
                total = total + dot2r(spread_ref[r], moved, NN)
            dw_ref[:, 0, first * count : first * count + N] = total


def grads_kernel(lens_ref, q_ref, k_ref, g_ref, ends_ref, u_ref, dx_ref, sum_ref, beta_ref, tw_ref,
                 dq_ref, dk_ref, dv_ref, dgate_ref,
                 linked_s, head_s, tail_s):
    ctx = lax.axis_index("ctx")

    @pl.when(pl.program_id(0) == 0)
    def _():
        linked_s[...], head_s[...], tail_s[...], unused = plan(lens_ref, ctx)

    linked, head, tail, tw = linked_s[...], head_s[...], tail_s[...], tw_ref[...]
    strict = jnp.where(iota(0) > iota(1), 1.0, 0.0)
    reach = iota(0) >= iota(1)
    last = jnp.where(lax.broadcasted_iota(jnp.int32, (N, 1), 0) == N - 1, 1.0, 0.0)
    for i in range(HG):
        h = pl.program_id(0) * HG + i
        cols = slice(i * N, (i + 1) * N)
        q, k, g = q_ref[:, cols], k_ref[:, cols], g_ref[:, cols]
        gate_row, beta_row = sum_ref[pl.ds(h, 1), :], beta_ref[pl.ds(h, 1), :]
        qn, kn, rq, rk, rk_cols, decay, key_key, query_key, from_head, to_tail, beta = head_terms(
            q, k, gate_row, beta_row, linked, head, tail)
        state, grad, u, dx = ends_ref[i, 0], ends_ref[i, 1], u_ref[i], dx_ref[i]
        pair = -(strict * beta * decay) * dot3(dx, u, NT)
        dqk = decay * (tw * dot2r(g, u, NT))
        dtail = dot3(u, grad, NN)
        gs = tw * dot2r(g, state, NN)
        dxs = dot3(dx, state, NN)
        both = dot2l(jnp.concatenate([dqk * rk_cols, (pair + pair.T) * rk_cols], axis=0), k, NN)
        dqn = from_head * gs + both[:N]
        dkn = dot2l(dqk * rq, q, TN) + to_tail * dtail - beta * from_head * dxs + both[N:]
        dq_ref[:, cols] = (rq * (dqn - qn * jnp.sum(dqn * qn, axis=1, keepdims=True))).astype(BF16)
        dk_ref[:, cols] = (rk * (dkn - kn * jnp.sum(dkn * kn, axis=1, keepdims=True))).astype(BF16)
        dv_ref[:, cols] = (beta * dx).astype(BF16)
        spread = dqk * query_key + pair * key_key
        tails = jnp.sum(to_tail * dtail * kn, axis=1, keepdims=True)
        heads = jnp.sum(from_head * (gs * qn - beta * dxs * kn), axis=1, keepdims=True)
        through = jnp.sum(from_head[N - 1 : N, :] * jnp.sum(state * grad, axis=0, keepdims=True), axis=1, keepdims=True)
        dgamma = jnp.sum(spread, axis=1, keepdims=True) + heads - tails
        dgamma = dgamma + last * (jnp.sum(tails, axis=0, keepdims=True) + through)
        dgamma = dgamma - by_row(jnp.sum(spread, axis=0, keepdims=True))
        dgate_ref[pl.ds(h, 1), :] = jnp.sum(jnp.where(reach, dgamma, 0.0), axis=0, keepdims=True)


def sum_kernel(parts_ref, out_ref, rows_s):
    heads, rows = out_ref.shape
    total = jnp.sum(parts_ref[:, 0, :], axis=0, keepdims=True)
    rows_s[...] = jnp.zeros((N, N), F32)
    for r in range(rows):
        rows_s[r : r + 1, :heads] = total[:, r * heads : (r + 1) * heads]
    out_ref[...] = rows_s[...].T[:heads, :rows]


def whole(shape):
    return pl.BlockSpec(shape, lambda i: (0,) * len(shape))


def to_owners(x):
    return lax.all_to_all(x, "ctx", 0, 0, tiled=True)


def local(queries, key_rows, value_rows, hidden_in, beta_weight, log_gate, out_grad, lengths, rewards, prompts):
    tokens, width = queries.shape
    depth, heads = beta_weight.shape
    parts = lax.axis_size("dp") * lax.axis_size("ctx")
    owned_rows = depth // parts
    tiles = -(-owned_rows * heads // N)
    smem = pl.BlockSpec(memory_space=pltpu.SMEM)
    by_heads = pl.BlockSpec((tokens, HP * N), lambda i: (0, i))
    params = pltpu.CompilerParams(vmem_limit_bytes=VMEM_LIMIT)
    prompts_row, rewards_row = prompts.reshape(1, -1), rewards.reshape(1, -1)

    def square(n):
        return pl.BlockSpec((HP, n, N, N), lambda i: (i, 0, 0, 0))

    one_square = pl.BlockSpec((HP, N, N), lambda i: (i, 0, 0))
    masks = [pltpu.VMEM((N, N), F32)] * 3
    maps, inverse, sums, beta, tw = pl.pallas_call(
        maps_kernel,
        grid=(heads // HP,),
        in_specs=[smem, smem, whole(rewards_row.shape), whole(prompts_row.shape), whole(log_gate.shape),
                  whole((heads, depth)), whole(hidden_in.shape)] + [by_heads] * 4,
        out_specs=[square(3), one_square, whole((heads, N)), whole((heads, N)), whole((N, N))],
        out_shape=[jax.ShapeDtypeStruct(s, F32) for s in (
            (heads, 3, N, N), (heads, N, N), (heads, N), (heads, N), (N, N))],
        scratch_shapes=masks,
        compiler_params=params,
        name="segment_maps",
    )(lengths, prompts_row, rewards_row, prompts_row, log_gate, beta_weight.T, hidden_in,
      queries, key_rows, value_rows, out_grad)
    owned = to_owners(maps)
    few_heads = pl.BlockSpec((tokens, HG * N), lambda i: (0, i))
    few_squares = pl.BlockSpec((HG, N, N), lambda i: (i, 0, 0))
    few_parts = pl.BlockSpec((HG, N, 2 * N), lambda i: (i, 0, 0))
    half = jax.ShapeDtypeStruct((heads, N, N), F32)
    in_parts = jax.ShapeDtypeStruct((heads, N, 2 * N), BF16)
    u0, z, dx0, x = pl.pallas_call(
        ahead_kernel,
        grid=(heads // HG,),
        in_specs=[smem] + [few_heads] * 4 + [few_squares, whole((heads, N)), whole((heads, N)), whole((N, N))],
        out_specs=[few_squares, few_parts] * 2,
        out_shape=[half, in_parts] * 2,
        scratch_shapes=masks,
        compiler_params=params,
        cost_estimate=pl.CostEstimate(flops=12_000_000_000, bytes_accessed=40_000_000, transcendentals=0),
        name="ahead",
    )(lengths, queries, key_rows, value_rows, out_grad, inverse, sums, beta, tw)
    ends = pl.pallas_call(
        chains_kernel,
        out_shape=jax.ShapeDtypeStruct((owned.shape[0], 2, N, N), F32),
        in_specs=[pl.BlockSpec(memory_space=pltpu.VMEM)],
        out_specs=pl.BlockSpec(memory_space=pltpu.VMEM),
        compiler_params=params,
        name="chains",
    )(owned)
    ends = to_owners(ends)
    spread = hidden_in.T.reshape(parts, owned_rows, tokens).transpose(1, 0, 2)
    parts_spec = pl.BlockSpec((HP, N, 2 * N), lambda i: (i, 0, 0))
    u, dx, dw = pl.pallas_call(
        logits_kernel,
        grid=(heads // HP,),
        in_specs=[square(2)] + [one_square, parts_spec] * 2 + [whole((heads, N)), whole(spread.shape)],
        out_specs=[one_square] * 2 + [whole((parts, 1, tiles * N))],
        out_shape=[half] * 2 + [jax.ShapeDtypeStruct((parts, 1, tiles * N), F32)],
        scratch_shapes=[pltpu.VMEM((N, N), F32)],
        compiler_params=params,
        name="logit_grads",
    )(ends, u0, z, dx0, x, beta, spread)
    pieces = lax.all_to_all(dw, ("dp", "ctx"), 0, 0, tiled=True)
    dq, dk, dv, dgate = pl.pallas_call(
        grads_kernel,
        grid=(heads // HG,),
        in_specs=[smem] + [few_heads] * 3 + [pl.BlockSpec((HG, 2, N, N), lambda i: (i, 0, 0, 0)), few_squares, few_squares,
                                             whole((heads, N)), whole((heads, N)), whole((N, N))],
        out_specs=[few_heads] * 3 + [whole((heads, N))],
        out_shape=[jax.ShapeDtypeStruct((tokens, width), BF16)] * 3 + [jax.ShapeDtypeStruct((heads, N), F32)],
        scratch_shapes=masks,
        compiler_params=params,
        cost_estimate=pl.CostEstimate(flops=12_000_000_000, bytes_accessed=40_000_000, transcendentals=0),
        name="segment_grads",
    )(lengths, queries, key_rows, out_grad, ends, u, dx, sums, beta, tw)
    dweight = pl.pallas_call(
        sum_kernel,
        out_shape=jax.ShapeDtypeStruct((heads, owned_rows), F32),
        in_specs=[pl.BlockSpec(memory_space=pltpu.VMEM)],
        out_specs=pl.BlockSpec(memory_space=pltpu.VMEM),
        scratch_shapes=[pltpu.VMEM((N, N), F32)],
        compiler_params=pltpu.CompilerParams(vmem_limit_bytes=VMEM_SMALL),
        name="sum_parts",
    )(pieces)
    return dq, dk, dv, dgate, dweight.T


def solution(mesh):
    rows = P(("dp", "ctx"), None)
    gates = P(None, ("dp", "ctx"))
    in_specs = (rows, rows, rows, rows, P(), gates, rows, P("dp", None), P(), P())
    out_specs = (rows, rows, rows, gates, rows)
    return jax.shard_map(local, mesh=mesh, in_specs=in_specs, out_specs=out_specs, check_vma=False)
```

```python
import jax
import jax.numpy as jnp
from jax import lax
from jax.experimental import pallas as pl
from jax.experimental.pallas import tpu as pltpu
from jax.sharding import PartitionSpec as P

F32 = jnp.float32
BF16 = jnp.bfloat16
N = 128
HP = 8
HL = 4
HG = 4
VMEM_LIMIT = 56 * 1024 * 1024
VMEM_MOST = 57 * 1024 * 1024
VMEM_SMALL = 24 * 1024 * 1024
NN = (((1,), (0,)), ((), ()))
NT = (((1,), (1,)), ((), ()))
TN = (((0,), (0,)), ((), ()))


def split(x):
    hi = x.astype(BF16)
    return hi, (x - hi.astype(F32)).astype(BF16)


def dot(a, b, dims):
    return lax.dot_general(a, b, dims, preferred_element_type=F32)


def dot3(a, b, dims):
    return parts_dot(jnp.concatenate(split(a), dims[0][0][0]), b, dims)


def parts_dot(a_parts, b, dims):
    kb = dims[0][1][0]
    n = b.shape[1 - kb]
    rights = jnp.concatenate(split(b), 1 - kb)
    both = dot(a_parts, jnp.concatenate([rights, rights], kb), dims)
    return both[:, :n] + both[:, n:]


def dot2l(a, b, dims):
    (ka,), (kb,) = dims[0]
    return dot(jnp.concatenate(split(a), ka), jnp.concatenate([b, b], kb), dims)


def dot2r(a, b, dims):
    (ka,), (kb,) = dims[0]
    return dot(jnp.concatenate([a, a], ka), jnp.concatenate(split(b), kb), dims)


def iota(axis):
    return lax.broadcasted_iota(jnp.int32, (N, N), axis)


def unit_inverses(lowers):
    rows, cols = iota(0), iota(1)
    same = jnp.where(rows == cols, 1.0, 0.0)
    pair = jnp.where(rows // 2 == cols // 2, 1.0, 0.0)
    inverses = [same - pair * lower for lower in lowers]
    size = 2
    while size < N:
        off = jnp.where((rows // (2 * size) == cols // (2 * size)) & (rows // size != cols // size), 1.0, 0.0)
        steps = [dot3(off * lower, inverse, NN) for lower, inverse in zip(lowers, inverses)]
        inverses = [inverse - dot3(inverse, step, NN) for inverse, step in zip(inverses, steps)]
        size *= 2
    return inverses


def begins_of(lens_ref):
    begins, at = [], jnp.int32(0)
    for i in range(lens_ref.shape[1]):
        begins.append(at)
        at = at + lens_ref[0, i]
    return begins


def plan(lens_ref, ctx):
    begins = begins_of(lens_ref)
    first = ctx * N
    row_pos, col_pos = iota(0) + first, iota(1) + first

    def count(at):
        return sum((b <= at).astype(jnp.int32) for b in begins)

    row_id, col_id = count(row_pos), count(col_pos)
    linked = jnp.where((row_id == col_id) & (row_pos >= col_pos), 1.0, 0.0)
    head = jnp.where(row_id == count(first - 1), 1.0, 0.0)
    tail = jnp.where(row_id == count(first + N - 1), 1.0, 0.0)
    return linked, head, tail, row_id


def token_weights(lens_ref, prompts_ref, rewards_row, prompts_row, row_id, dp):
    rolls = lens_ref.shape[1]
    lanes = lax.broadcasted_iota(jnp.int32, rewards_row.shape, 1)
    weight = jnp.zeros((N, N), F32)
    for i in range(rolls):
        at = dp * rolls + i
        same = jnp.where(prompts_row == prompts_ref[0, at], 1.0, 0.0)
        mean = jnp.sum(same * rewards_row, axis=1, keepdims=True) / jnp.sum(same, axis=1, keepdims=True)
        own = jnp.sum(jnp.where(lanes == at, rewards_row, 0.0), axis=1, keepdims=True)
        length = jnp.full((1, 1), lens_ref[0, i], jnp.int32).astype(F32)
        scale = (own - mean) * (16.0 * N) / (rolls * length)
        weight = jnp.where(row_id == i + 1, scale, weight)
    return weight


def inverse_norm(rows):
    total = jnp.sum(rows * rows, axis=1, keepdims=True)
    return jnp.broadcast_to(lax.rsqrt(total + 1e-06), (N, N))


def by_row(row):
    return jnp.broadcast_to(row, (N, N)).T


def head_terms(q, k, gate_row, beta_row, linked, head, tail):
    qf, kf = q.astype(F32), k.astype(F32)
    rq, rk = inverse_norm(qf), inverse_norm(kf)
    rk_cols = rk.T
    gate = by_row(gate_row)
    decay = jnp.exp(jnp.minimum(gate - gate_row, 0.0)) * linked
    pairs = dot(jnp.concatenate([k, q], axis=0), k, NT)
    key_key = pairs[:N] * rk * rk_cols
    query_key = pairs[N:] * rq * rk_cols
    from_head = head * jnp.exp(gate)
    to_tail = tail * jnp.exp(gate[N - 1 : N, :] - gate)
    return qf * rq, kf * rk, rq, rk, rk_cols, decay, key_key, query_key, from_head, to_tail, by_row(beta_row)


def maps_kernel(lens_ref, prompts_ref, rewards_row_ref, prompts_row_ref, gate_ref, weight_ref, hidden_ref,
                q_ref, k_ref, v_ref, g_ref,
                maps_ref, inv_ref, sum_ref, beta_ref, tw_ref,
                linked_s, head_s, tail_s):
    ctx, dp = lax.axis_index("ctx"), lax.axis_index("dp")

    @pl.when(pl.program_id(0) == 0)
    def _():
        linked, head, tail, row_id = plan(lens_ref, ctx)
        linked_s[...], head_s[...], tail_s[...] = linked, head, tail
        tw_ref[...] = token_weights(lens_ref, prompts_ref, rewards_row_ref[...], prompts_row_ref[...], row_id, dp)
        logits = dot(weight_ref[...], hidden_ref[...], NT)
        beta_ref[...] = 1.0 / (1.0 + jnp.exp(-logits))
        upto = jnp.where(iota(0) <= iota(1), 1.0, 0.0).astype(BF16)
        gates = gate_ref[...]
        hi, rest = split(gates)
        mid = gates - hi.astype(F32)
        mid, low = split(mid)
        sum_ref[...] = dot(hi, upto, NN) + (dot(mid, upto, NN) + dot(low, upto, NN))

    linked, head, tail, tw = linked_s[...], head_s[...], tail_s[...], tw_ref[...]
    strict = jnp.where(iota(0) > iota(1), 1.0, 0.0)
    same = jnp.where(iota(0) == iota(1), 1.0, 0.0)
    lowers, rest, mgs = [], [], []
    for i in range(HP):
        h = pl.program_id(0) * HP + i
        cols = slice(i * N, (i + 1) * N)
        q, k, v, g = q_ref[:, cols], k_ref[:, cols], v_ref[:, cols], g_ref[:, cols]
        gate_row, beta_row = sum_ref[pl.ds(h, 1), :], beta_ref[pl.ds(h, 1), :]
        qn, kn, rq, rk, rk_cols, decay, key_key, query_key, from_head, to_tail, beta = head_terms(
            q, k, gate_row, beta_row, linked, head, tail)
        lowers.append(strict * (beta * decay * key_key))
        mgs.append(dot2l(decay * query_key * tw, g, TN))
        maps_ref[i, 2] = dot2r(g, tw * from_head * qn, TN)
        maps_ref[i, 0] = from_head[N - 1 : N, :] * same
        rest.append((jnp.concatenate([beta * v.astype(F32), beta * from_head * kn], axis=1), to_tail * kn))
    inverses = unit_inverses(lowers)
    for i in range(HP):
        inv_ref[i] = inverses[i]
    uzs = [dot3(inverse, sides, NN) for inverse, (sides, _) in zip(inverses, rest)]
    for i in range(HP):
        ends = dot3(uzs[i], rest[i][1], TN)
        maps_ref[i, 0] -= ends[N:]
        maps_ref[i, 1] = ends[:N]
        maps_ref[i, 2] -= dot3(mgs[i], uzs[i][:, N:], TN)


def chains_kernel(maps_any, out_any, maps_v, out_v, in_sem, out_sem):
    count = maps_any.shape[0]
    loads = [pltpu.make_async_copy(maps_any.at[j], maps_v.at[j], in_sem.at[j]) for j in range(count)]
    for j in range(count // 2):
        loads[j].start()
        loads[count - 1 - j].start()
    state = jnp.zeros((N, N), F32)
    grad = jnp.zeros((N, N), F32)
    stores = []
    for j in range(count):
        b = count - 1 - j
        out_v[j, 0] = state
        out_v[b, 1] = grad
        for at, kind in ((j, 0), (b, 1)):
            stores.append(pltpu.make_async_copy(out_v.at[at, kind], out_any.at[at, kind], out_sem.at[at, kind]))
            stores[-1].start()
        if j < count // 2:
            loads[j].wait()
            loads[b].wait()
        if j < count - 1:
            state = dot3(state, maps_v[j, 0], NN) + maps_v[j, 1]
            grad = dot3(grad, maps_v[b, 0], NT) + maps_v[b, 2]
    for store in stores:
        store.wait()


def ahead_kernel(lens_ref, q_ref, k_ref, v_ref, g_ref, inv_ref, sum_ref, beta_ref, tw_ref,
                 u0_ref, z_ref, dx0_ref, x_ref,
                 linked_s, head_s, tail_s):
    ctx = lax.axis_index("ctx")

    @pl.when(pl.program_id(0) == 0)
    def _():
        linked_s[...], head_s[...], tail_s[...], unused = plan(lens_ref, ctx)

    linked, head, tail, tw = linked_s[...], head_s[...], tail_s[...], tw_ref[...]
    for i in range(HG):
        h = pl.program_id(0) * HG + i
        cols = slice(i * N, (i + 1) * N)
        q, k, v, g = q_ref[:, cols], k_ref[:, cols], v_ref[:, cols], g_ref[:, cols]
        gate_row, beta_row = sum_ref[pl.ds(h, 1), :], beta_ref[pl.ds(h, 1), :]
        qn, kn, rq, rk, rk_cols, decay, key_key, query_key, from_head, to_tail, beta = head_terms(
            q, k, gate_row, beta_row, linked, head, tail)
        uz = dot3(inv_ref[i], jnp.concatenate([beta * v.astype(F32), beta * from_head * kn], axis=1), NN)
        u0_ref[i] = uz[:, :N]
        z_ref[i] = jnp.concatenate(split(uz[:, N:]), axis=1)
        mg = dot2l(decay * query_key * tw, g, TN)
        dxx = dot3(inv_ref[i], jnp.concatenate([mg, to_tail * kn], axis=1), TN)
        dx0_ref[i] = dxx[:, :N]
        x_ref[i] = jnp.concatenate(split(dxx[:, N:]), axis=1)


def logits_kernel(ends_any, u0_any, z_any, dx0_any, x_any, beta_ref, spread_ref,
                  u_any, dx_any, dw_ref,
                  ends_v, u0_v, z_v, dx0_v, x_v, u_v, dx_v, in_sem, out_sem):
    heads = beta_ref.shape[0]
    groups = heads // HL
    sources = ((ends_any, ends_v), (u0_any, u0_v), (z_any, z_v), (dx0_any, dx0_v), (x_any, x_v))
    loads, stores = [], []
    for c in range(groups):
        at = pl.ds(c * HL, HL)
        loads.append([pltpu.make_async_copy(a.at[at], v.at[at], in_sem.at[c, n]) for n, (a, v) in enumerate(sources)])
        for load in loads[-1]:
            load.start()
    sums = jnp.zeros((N, N), F32)
    for c in range(groups):
        for load in loads[c]:
            load.wait()
        for i in range(c * HL, c * HL + HL):
            u = u0_v[i] - parts_dot(z_v[i], ends_v[i, 0], NT)
            dx = dx0_v[i] + parts_dot(x_v[i], ends_v[i, 1], NT)
            u_v[i], dx_v[i] = u, dx
            sums = jnp.where(iota(1) == i, jnp.sum(dx * u, axis=1, keepdims=True), sums)
        at = pl.ds(c * HL, HL)
        for n, (v, a) in enumerate(((u_v, u_any), (dx_v, dx_any))):
            stores.append(pltpu.make_async_copy(v.at[at], a.at[at], out_sem.at[c, n]))
            stores[-1].start()
    dlogit = sums * (1.0 - jnp.concatenate([beta_ref[...], jnp.zeros((N - heads, N), F32)], axis=0).T)
    per = N // heads
    rows = spread_ref.shape[0]
    for first in range(0, rows, per):
        total = jnp.zeros((N, N), F32)
        for r in range(first, min(first + per, rows)):
            moved = dlogit if r == first else pltpu.roll(dlogit, heads * (r - first), 1)
            total = total + dot2r(spread_ref[r], moved, NN)
        dw_ref[:, 0, first * heads : first * heads + N] = total
    for store in stores:
        store.wait()


def grads_kernel(lens_ref, q_ref, k_ref, g_ref, ends_ref, u_ref, dx_ref, sum_ref, beta_ref, tw_ref,
                 dq_ref, dk_ref, dv_ref, dgate_ref,
                 linked_s, head_s, tail_s):
    ctx = lax.axis_index("ctx")

    @pl.when(pl.program_id(0) == 0)
    def _():
        linked_s[...], head_s[...], tail_s[...], unused = plan(lens_ref, ctx)

    linked, head, tail, tw = linked_s[...], head_s[...], tail_s[...], tw_ref[...]
    strict = jnp.where(iota(0) > iota(1), 1.0, 0.0)
    reach = iota(0) >= iota(1)
    last = jnp.where(lax.broadcasted_iota(jnp.int32, (N, 1), 0) == N - 1, 1.0, 0.0)
    for i in range(HG):
        h = pl.program_id(0) * HG + i
        cols = slice(i * N, (i + 1) * N)
        q, k, g = q_ref[:, cols], k_ref[:, cols], g_ref[:, cols]
        gate_row, beta_row = sum_ref[pl.ds(h, 1), :], beta_ref[pl.ds(h, 1), :]
        qn, kn, rq, rk, rk_cols, decay, key_key, query_key, from_head, to_tail, beta = head_terms(
            q, k, gate_row, beta_row, linked, head, tail)
        state, grad, u, dx = ends_ref[i, 0], ends_ref[i, 1], u_ref[i], dx_ref[i]
        pair = -(strict * beta * decay) * dot3(dx, u, NT)
        dqk = decay * (tw * dot2r(g, u, NT))
        dtail = dot3(u, grad, NN)
        gs = tw * dot2r(g, state, NN)
        dxs = dot3(dx, state, NN)
        both = dot2l(jnp.concatenate([dqk * rk_cols, (pair + pair.T) * rk_cols], axis=0), k, NN)
        dqn = from_head * gs + both[:N]
        dkn = dot2l(dqk * rq, q, TN) + to_tail * dtail - beta * from_head * dxs + both[N:]
        dq_ref[:, cols] = (rq * (dqn - qn * jnp.sum(dqn * qn, axis=1, keepdims=True))).astype(BF16)
        dk_ref[:, cols] = (rk * (dkn - kn * jnp.sum(dkn * kn, axis=1, keepdims=True))).astype(BF16)
        dv_ref[:, cols] = (beta * dx).astype(BF16)
        spread = dqk * query_key + pair * key_key
        tails = jnp.sum(to_tail * dtail * kn, axis=1, keepdims=True)
        heads = jnp.sum(from_head * (gs * qn - beta * dxs * kn), axis=1, keepdims=True)
        through = jnp.sum(from_head[N - 1 : N, :] * jnp.sum(state * grad, axis=0, keepdims=True), axis=1, keepdims=True)
        dgamma = jnp.sum(spread, axis=1, keepdims=True) + heads - tails
        dgamma = dgamma + last * (jnp.sum(tails, axis=0, keepdims=True) + through)
        dgamma = dgamma - by_row(jnp.sum(spread, axis=0, keepdims=True))
        dgate_ref[pl.ds(h, 1), :] = jnp.sum(jnp.where(reach, dgamma, 0.0), axis=0, keepdims=True)


def sum_kernel(parts_ref, out_ref, rows_s):
    heads, rows = out_ref.shape
    total = jnp.sum(parts_ref[:, 0, :], axis=0, keepdims=True)
    rows_s[...] = jnp.zeros((N, N), F32)
    for r in range(rows):
        rows_s[r : r + 1, :heads] = total[:, r * heads : (r + 1) * heads]
    out_ref[...] = rows_s[...].T[:heads, :rows]


def whole(shape):
    return pl.BlockSpec(shape, lambda i: (0,) * len(shape))


def to_owners(x):
    return lax.all_to_all(x, "ctx", 0, 0, tiled=True)


def local(queries, key_rows, value_rows, hidden_in, beta_weight, log_gate, out_grad, lengths, rewards, prompts):
    tokens, width = queries.shape
    depth, heads = beta_weight.shape
    parts = lax.axis_size("dp") * lax.axis_size("ctx")
    owned_rows = depth // parts
    tiles = -(-owned_rows * heads // N)
    smem = pl.BlockSpec(memory_space=pltpu.SMEM)
    by_heads = pl.BlockSpec((tokens, HP * N), lambda i: (0, i))
    params = pltpu.CompilerParams(vmem_limit_bytes=VMEM_LIMIT)
    prompts_row, rewards_row = prompts.reshape(1, -1), rewards.reshape(1, -1)

    def square(n):
        return pl.BlockSpec((HP, n, N, N), lambda i: (i, 0, 0, 0))

    one_square = pl.BlockSpec((HP, N, N), lambda i: (i, 0, 0))
    masks = [pltpu.VMEM((N, N), F32)] * 3
    maps, inverse, sums, beta, tw = pl.pallas_call(
        maps_kernel,
        grid=(heads // HP,),
        in_specs=[smem, smem, whole(rewards_row.shape), whole(prompts_row.shape), whole(log_gate.shape),
                  whole((heads, depth)), whole(hidden_in.shape)] + [by_heads] * 4,
        out_specs=[square(3), one_square, whole((heads, N)), whole((heads, N)), whole((N, N))],
        out_shape=[jax.ShapeDtypeStruct(s, F32) for s in (
            (heads, 3, N, N), (heads, N, N), (heads, N), (heads, N), (N, N))],
        scratch_shapes=masks,
        compiler_params=params,
        name="segment_maps",
    )(lengths, prompts_row, rewards_row, prompts_row, log_gate, beta_weight.T, hidden_in,
      queries, key_rows, value_rows, out_grad)
    owned = to_owners(maps)
    few_heads = pl.BlockSpec((tokens, HG * N), lambda i: (0, i))
    few_squares = pl.BlockSpec((HG, N, N), lambda i: (i, 0, 0))
    few_parts = pl.BlockSpec((HG, N, 2 * N), lambda i: (i, 0, 0))
    half = jax.ShapeDtypeStruct((heads, N, N), F32)
    in_parts = jax.ShapeDtypeStruct((heads, N, 2 * N), BF16)
    u0, z, dx0, x = pl.pallas_call(
        ahead_kernel,
        grid=(heads // HG,),
        in_specs=[smem] + [few_heads] * 4 + [few_squares, whole((heads, N)), whole((heads, N)), whole((N, N))],
        out_specs=[few_squares, few_parts] * 2,
        out_shape=[half, in_parts] * 2,
        scratch_shapes=masks,
        compiler_params=params,
        cost_estimate=pl.CostEstimate(flops=12_000_000_000, bytes_accessed=40_000_000, transcendentals=0),
        name="ahead",
    )(lengths, queries, key_rows, value_rows, out_grad, inverse, sums, beta, tw)
    anywhere = pl.BlockSpec(memory_space=pl.ANY)
    count = owned.shape[0]
    ends = pl.pallas_call(
        chains_kernel,
        out_shape=jax.ShapeDtypeStruct((count, 2, N, N), F32),
        in_specs=[anywhere],
        out_specs=anywhere,
        scratch_shapes=[pltpu.VMEM((count, 3, N, N), F32), pltpu.VMEM((count, 2, N, N), F32),
                        pltpu.SemaphoreType.DMA((count,)), pltpu.SemaphoreType.DMA((count, 2))],
        compiler_params=pltpu.CompilerParams(vmem_limit_bytes=VMEM_SMALL),
        name="chains",
    )(owned)
    ends = to_owners(ends)
    spread = hidden_in.T.reshape(parts, owned_rows, tokens).transpose(1, 0, 2)
    vmem = pl.BlockSpec(memory_space=pltpu.VMEM)
    kept = pl.BlockSpec(memory_space=pl.ANY)
    u, dx, dw = pl.pallas_call(
        logits_kernel,
        in_specs=[anywhere] + [kept] * 4 + [vmem] * 2,
        out_specs=[kept] * 2 + [vmem],
        out_shape=[half] * 2 + [jax.ShapeDtypeStruct((parts, 1, tiles * N), F32)],
        scratch_shapes=[pltpu.VMEM((heads, 2, N, N), F32)]
        + [pltpu.VMEM((heads, N, N), F32), pltpu.VMEM((heads, N, 2 * N), BF16)] * 2
        + [pltpu.VMEM((heads, N, N), F32)] * 2
        + [pltpu.SemaphoreType.DMA((heads // HL, 5)), pltpu.SemaphoreType.DMA((heads // HL, 2))],
        compiler_params=pltpu.CompilerParams(vmem_limit_bytes=VMEM_MOST),
        name="logit_grads",
    )(ends, u0, z, dx0, x, beta, spread)
    pieces = lax.all_to_all(dw, ("dp", "ctx"), 0, 0, tiled=True)
    dq, dk, dv, dgate = pl.pallas_call(
        grads_kernel,
        grid=(heads // HG,),
        in_specs=[smem] + [few_heads] * 3 + [pl.BlockSpec((HG, 2, N, N), lambda i: (i, 0, 0, 0)), few_squares, few_squares,
                                             whole((heads, N)), whole((heads, N)), whole((N, N))],
        out_specs=[few_heads] * 3 + [whole((heads, N))],
        out_shape=[jax.ShapeDtypeStruct((tokens, width), BF16)] * 3 + [jax.ShapeDtypeStruct((heads, N), F32)],
        scratch_shapes=masks,
        compiler_params=params,
        cost_estimate=pl.CostEstimate(flops=12_000_000_000, bytes_accessed=40_000_000, transcendentals=0),
        name="segment_grads",
    )(lengths, queries, key_rows, out_grad, ends, u, dx, sums, beta, tw)
    dweight = pl.pallas_call(
        sum_kernel,
        out_shape=jax.ShapeDtypeStruct((heads, owned_rows), F32),
        in_specs=[pl.BlockSpec(memory_space=pltpu.VMEM)],
        out_specs=pl.BlockSpec(memory_space=pltpu.VMEM),
        scratch_shapes=[pltpu.VMEM((N, N), F32)],
        compiler_params=pltpu.CompilerParams(vmem_limit_bytes=VMEM_SMALL),
        name="sum_parts",
    )(pieces)
    return dq, dk, dv, dgate, dweight.T


def solution(mesh):
    rows = P(("dp", "ctx"), None)
    gates = P(None, ("dp", "ctx"))
    in_specs = (rows, rows, rows, rows, P(), gates, rows, P("dp", None), P(), P())
    out_specs = (rows, rows, rows, gates, rows)
    return jax.shard_map(local, mesh=mesh, in_specs=in_specs, out_specs=out_specs, check_vma=False)
```

```python
import jax
import jax.numpy as jnp
from jax import lax
from jax.experimental import pallas as pl
from jax.experimental.pallas import tpu as pltpu
from jax.sharding import PartitionSpec as P

F32 = jnp.float32
BF16 = jnp.bfloat16
N = 128
HP = 8
HG = 4
VMEM_LIMIT = 56 * 1024 * 1024
VMEM_SMALL = 24 * 1024 * 1024
NN = (((1,), (0,)), ((), ()))
NT = (((1,), (1,)), ((), ()))
TN = (((0,), (0,)), ((), ()))


def split(x):
    hi = x.astype(BF16)
    return hi, (x - hi.astype(F32)).astype(BF16)


def dot(a, b, dims):
    return lax.dot_general(a, b, dims, preferred_element_type=F32)


def dot3(a, b, dims):
    return parts_dot(jnp.concatenate(split(a), dims[0][0][0]), b, dims)


def parts_dot(a_parts, b, dims):
    kb = dims[0][1][0]
    n = b.shape[1 - kb]
    rights = jnp.concatenate(split(b), 1 - kb)
    both = dot(a_parts, jnp.concatenate([rights, rights], kb), dims)
    return both[:, :n] + both[:, n:]


def dot2l(a, b, dims):
    (ka,), (kb,) = dims[0]
    return dot(jnp.concatenate(split(a), ka), jnp.concatenate([b, b], kb), dims)


def dot2r(a, b, dims):
    (ka,), (kb,) = dims[0]
    return dot(jnp.concatenate([a, a], ka), jnp.concatenate(split(b), kb), dims)


def iota(axis):
    return lax.broadcasted_iota(jnp.int32, (N, N), axis)


def unit_inverses(lowers):
    rows, cols = iota(0), iota(1)
    same = jnp.where(rows == cols, 1.0, 0.0)
    pair = jnp.where(rows // 2 == cols // 2, 1.0, 0.0)
    inverses = [same - pair * lower for lower in lowers]
    size = 2
    while size < N:
        off = jnp.where((rows // (2 * size) == cols // (2 * size)) & (rows // size != cols // size), 1.0, 0.0)
        steps = [dot3(off * lower, inverse, NN) for lower, inverse in zip(lowers, inverses)]
        inverses = [inverse - dot3(inverse, step, NN) for inverse, step in zip(inverses, steps)]
        size *= 2
    return inverses


def begins_of(lens_ref):
    begins, at = [], jnp.int32(0)
    for i in range(lens_ref.shape[1]):
        begins.append(at)
        at = at + lens_ref[0, i]
    return begins


def plan(lens_ref, ctx):
    begins = begins_of(lens_ref)
    first = ctx * N
    row_pos, col_pos = iota(0) + first, iota(1) + first

    def count(at):
        return sum((b <= at).astype(jnp.int32) for b in begins)

    row_id, col_id = count(row_pos), count(col_pos)
    linked = jnp.where((row_id == col_id) & (row_pos >= col_pos), 1.0, 0.0)
    head = jnp.where(row_id == count(first - 1), 1.0, 0.0)
    tail = jnp.where(row_id == count(first + N - 1), 1.0, 0.0)
    return linked, head, tail, row_id


def token_weights(lens_ref, prompts_ref, rewards_row, prompts_row, row_id, dp):
    rolls = lens_ref.shape[1]
    lanes = lax.broadcasted_iota(jnp.int32, rewards_row.shape, 1)
    weight = jnp.zeros((N, N), F32)
    for i in range(rolls):
        at = dp * rolls + i
        same = jnp.where(prompts_row == prompts_ref[0, at], 1.0, 0.0)
        mean = jnp.sum(same * rewards_row, axis=1, keepdims=True) / jnp.sum(same, axis=1, keepdims=True)
        own = jnp.sum(jnp.where(lanes == at, rewards_row, 0.0), axis=1, keepdims=True)
        length = jnp.full((1, 1), lens_ref[0, i], jnp.int32).astype(F32)
        scale = (own - mean) * (16.0 * N) / (rolls * length)
        weight = jnp.where(row_id == i + 1, scale, weight)
    return weight


def inverse_norm(rows):
    total = jnp.sum(rows * rows, axis=1, keepdims=True)
    return jnp.broadcast_to(lax.rsqrt(total + 1e-06), (N, N))


def by_row(row):
    return jnp.broadcast_to(row, (N, N)).T


def head_terms(q, k, gate_row, beta_row, linked, head, tail):
    qf, kf = q.astype(F32), k.astype(F32)
    rq, rk = inverse_norm(qf), inverse_norm(kf)
    rk_cols = rk.T
    gate = by_row(gate_row)
    decay = jnp.exp(jnp.minimum(gate - gate_row, 0.0)) * linked
    pairs = dot(jnp.concatenate([k, q], axis=0), k, NT)
    key_key = pairs[:N] * rk * rk_cols
    query_key = pairs[N:] * rq * rk_cols
    from_head = head * jnp.exp(gate)
    to_tail = tail * jnp.exp(gate[N - 1 : N, :] - gate)
    return qf * rq, kf * rk, rq, rk, rk_cols, decay, key_key, query_key, from_head, to_tail, by_row(beta_row)


def maps_kernel(lens_ref, prompts_ref, rewards_row_ref, prompts_row_ref, gate_ref, weight_ref, hidden_ref,
                q_ref, k_ref, v_ref, g_ref,
                maps_ref, inv_ref, sum_ref, beta_ref, tw_ref,
                linked_s, head_s, tail_s):
    ctx, dp = lax.axis_index("ctx"), lax.axis_index("dp")

    @pl.when(pl.program_id(0) == 0)
    def _():
        linked, head, tail, row_id = plan(lens_ref, ctx)
        linked_s[...], head_s[...], tail_s[...] = linked, head, tail
        tw_ref[...] = token_weights(lens_ref, prompts_ref, rewards_row_ref[...], prompts_row_ref[...], row_id, dp)
        logits = dot(weight_ref[...], hidden_ref[...], NT)
        beta_ref[...] = 1.0 / (1.0 + jnp.exp(-logits))
        upto = jnp.where(iota(0) <= iota(1), 1.0, 0.0).astype(BF16)
        gates = gate_ref[...]
        hi, rest = split(gates)
        mid = gates - hi.astype(F32)
        mid, low = split(mid)
        sum_ref[...] = dot(hi, upto, NN) + (dot(mid, upto, NN) + dot(low, upto, NN))

    linked, head, tail, tw = linked_s[...], head_s[...], tail_s[...], tw_ref[...]
    strict = jnp.where(iota(0) > iota(1), 1.0, 0.0)
    same = jnp.where(iota(0) == iota(1), 1.0, 0.0)
    lowers, rest, mgs = [], [], []
    for i in range(HP):
        h = pl.program_id(0) * HP + i
        cols = slice(i * N, (i + 1) * N)
        q, k, v, g = q_ref[:, cols], k_ref[:, cols], v_ref[:, cols], g_ref[:, cols]
        gate_row, beta_row = sum_ref[pl.ds(h, 1), :], beta_ref[pl.ds(h, 1), :]
        qn, kn, rq, rk, rk_cols, decay, key_key, query_key, from_head, to_tail, beta = head_terms(
            q, k, gate_row, beta_row, linked, head, tail)
        lowers.append(strict * (beta * decay * key_key))
        mgs.append(dot2l(decay * query_key * tw, g, TN))
        maps_ref[i, 2] = dot2r(g, tw * from_head * qn, TN)
        maps_ref[i, 0] = from_head[N - 1 : N, :] * same
        rest.append((jnp.concatenate([beta * v.astype(F32), beta * from_head * kn], axis=1), to_tail * kn))
    inverses = unit_inverses(lowers)
    for i in range(HP):
        inv_ref[i] = inverses[i]
    uzs = [dot3(inverse, sides, NN) for inverse, (sides, _) in zip(inverses, rest)]
    for i in range(HP):
        ends = dot3(uzs[i], rest[i][1], TN)
        maps_ref[i, 0] -= ends[N:]
        maps_ref[i, 1] = ends[:N]
        maps_ref[i, 2] -= dot3(mgs[i], uzs[i][:, N:], TN)


def chains_kernel(maps_ref, out_ref):
    count = maps_ref.shape[0]
    state = jnp.zeros((N, N), F32)
    grad = jnp.zeros((N, N), F32)
    for j in range(count):
        b = count - 1 - j
        out_ref[j, 0] = state
        out_ref[b, 1] = grad
        if j < count - 1:
            state = dot3(state, maps_ref[j, 0], NN) + maps_ref[j, 1]
            grad = dot3(grad, maps_ref[b, 0], NT) + maps_ref[b, 2]


def ahead_kernel(lens_ref, q_ref, k_ref, v_ref, g_ref, inv_ref, sum_ref, beta_ref, tw_ref,
                 u0_ref, z_ref, dx0_ref, x_ref,
                 linked_s, head_s, tail_s):
    ctx = lax.axis_index("ctx")

    @pl.when(pl.program_id(0) == 0)
    def _():
        linked_s[...], head_s[...], tail_s[...], unused = plan(lens_ref, ctx)

    linked, head, tail, tw = linked_s[...], head_s[...], tail_s[...], tw_ref[...]
    for i in range(HG):
        h = pl.program_id(0) * HG + i
        cols = slice(i * N, (i + 1) * N)
        q, k, v, g = q_ref[:, cols], k_ref[:, cols], v_ref[:, cols], g_ref[:, cols]
        gate_row, beta_row = sum_ref[pl.ds(h, 1), :], beta_ref[pl.ds(h, 1), :]
        qn, kn, rq, rk, rk_cols, decay, key_key, query_key, from_head, to_tail, beta = head_terms(
            q, k, gate_row, beta_row, linked, head, tail)
        uz = dot3(inv_ref[i], jnp.concatenate([beta * v.astype(F32), beta * from_head * kn], axis=1), NN)
        u0_ref[i] = uz[:, :N]
        z_ref[i] = jnp.concatenate(split(uz[:, N:]), axis=1)
        mg = dot2l(decay * query_key * tw, g, TN)
        dxx = dot3(inv_ref[i], jnp.concatenate([mg, to_tail * kn], axis=1), TN)
        dx0_ref[i] = dxx[:, :N]
        x_ref[i] = jnp.concatenate(split(dxx[:, N:]), axis=1)


def logits_kernel(ends_ref, u0_ref, z_ref, dx0_ref, x_ref, beta_ref, spread_ref,
                  u_ref, dx_ref, dw_ref, sums_s):
    @pl.when(pl.program_id(0) == 0)
    def _():
        sums_s[...] = jnp.zeros((N, N), F32)

    sums = sums_s[...]
    for i in range(HP):
        u = u0_ref[i] - parts_dot(z_ref[i], ends_ref[i, 0], NT)
        dx = dx0_ref[i] + parts_dot(x_ref[i], ends_ref[i, 1], NT)
        u_ref[i], dx_ref[i] = u, dx
        sums = jnp.where(iota(1) == pl.program_id(0) * HP + i, jnp.sum(dx * u, axis=1, keepdims=True), sums)
    sums_s[...] = sums

    @pl.when(pl.program_id(0) == pl.num_programs(0) - 1)
    def _():
        count = beta_ref.shape[0]
        dlogit = sums * (1.0 - jnp.concatenate([beta_ref[...], jnp.zeros((N - count, N), F32)], axis=0).T)
        per = N // count
        rows = spread_ref.shape[0]
        for first in range(0, rows, per):
            total = jnp.zeros((N, N), F32)
            for r in range(first, min(first + per, rows)):
                moved = dlogit if r == first else pltpu.roll(dlogit, count * (r - first), 1)
                total = total + dot2r(spread_ref[r], moved, NN)
            dw_ref[:, 0, first * count : first * count + N] = total


def grads_kernel(lens_ref, q_ref, k_ref, g_ref, ends_ref, u_ref, dx_ref, sum_ref, beta_ref, tw_ref,
                 dq_ref, dk_ref, dv_ref, dgate_ref,
                 linked_s, head_s, tail_s):
    ctx = lax.axis_index("ctx")

    @pl.when(pl.program_id(0) == 0)
    def _():
        linked_s[...], head_s[...], tail_s[...], unused = plan(lens_ref, ctx)

    linked, head, tail, tw = linked_s[...], head_s[...], tail_s[...], tw_ref[...]
    strict = jnp.where(iota(0) > iota(1), 1.0, 0.0)
    reach = iota(0) >= iota(1)
    last = jnp.where(lax.broadcasted_iota(jnp.int32, (N, 1), 0) == N - 1, 1.0, 0.0)
    for i in range(HG):
        h = pl.program_id(0) * HG + i
        cols = slice(i * N, (i + 1) * N)
        q, k, g = q_ref[:, cols], k_ref[:, cols], g_ref[:, cols]
        gate_row, beta_row = sum_ref[pl.ds(h, 1), :], beta_ref[pl.ds(h, 1), :]
        qn, kn, rq, rk, rk_cols, decay, key_key, query_key, from_head, to_tail, beta = head_terms(
            q, k, gate_row, beta_row, linked, head, tail)
        state, grad, u, dx = ends_ref[i, 0], ends_ref[i, 1], u_ref[i], dx_ref[i]
        pair = -(strict * beta * decay) * dot3(dx, u, NT)
        dqk = decay * (tw * dot2r(g, u, NT))
        dtail = dot3(u, grad, NN)
        gs = tw * dot2r(g, state, NN)
        dxs = dot3(dx, state, NN)
        both = dot2l(jnp.concatenate([dqk * rk_cols, (pair + pair.T) * rk_cols], axis=0), k, NN)
        dqn = from_head * gs + both[:N]
        dkn = dot2l(dqk * rq, q, TN) + to_tail * dtail - beta * from_head * dxs + both[N:]
        dq_ref[:, cols] = (rq * (dqn - qn * jnp.sum(dqn * qn, axis=1, keepdims=True))).astype(BF16)
        dk_ref[:, cols] = (rk * (dkn - kn * jnp.sum(dkn * kn, axis=1, keepdims=True))).astype(BF16)
        dv_ref[:, cols] = (beta * dx).astype(BF16)
        spread = dqk * query_key + pair * key_key
        tails = jnp.sum(to_tail * dtail * kn, axis=1, keepdims=True)
        heads = jnp.sum(from_head * (gs * qn - beta * dxs * kn), axis=1, keepdims=True)
        through = jnp.sum(from_head[N - 1 : N, :] * jnp.sum(state * grad, axis=0, keepdims=True), axis=1, keepdims=True)
        dgamma = jnp.sum(spread, axis=1, keepdims=True) + heads - tails
        dgamma = dgamma + last * (jnp.sum(tails, axis=0, keepdims=True) + through)
        dgamma = dgamma - by_row(jnp.sum(spread, axis=0, keepdims=True))
        dgate_ref[pl.ds(h, 1), :] = jnp.sum(jnp.where(reach, dgamma, 0.0), axis=0, keepdims=True)


def sum_kernel(parts_ref, out_ref, rows_s):
    heads, rows = out_ref.shape
    total = jnp.sum(parts_ref[:, 0, :], axis=0, keepdims=True)
    rows_s[...] = jnp.zeros((N, N), F32)
    for r in range(rows):
        rows_s[r : r + 1, :heads] = total[:, r * heads : (r + 1) * heads]
    out_ref[...] = rows_s[...].T[:heads, :rows]


def whole(shape):
    return pl.BlockSpec(shape, lambda i: (0,) * len(shape))


def to_owners(x):
    return lax.all_to_all(x, "ctx", 0, 0, tiled=True)


def local(queries, key_rows, value_rows, hidden_in, beta_weight, log_gate, out_grad, lengths, rewards, prompts):
    tokens, width = queries.shape
    depth, heads = beta_weight.shape
    parts = lax.axis_size("dp") * lax.axis_size("ctx")
    owned_rows = depth // parts
    tiles = -(-owned_rows * heads // N)
    smem = pl.BlockSpec(memory_space=pltpu.SMEM)
    by_heads = pl.BlockSpec((tokens, HP * N), lambda i: (0, i))
    params = pltpu.CompilerParams(vmem_limit_bytes=VMEM_LIMIT)
    prompts_row, rewards_row = prompts.reshape(1, -1), rewards.reshape(1, -1)

    def square(n):
        return pl.BlockSpec((HP, n, N, N), lambda i: (i, 0, 0, 0))

    one_square = pl.BlockSpec((HP, N, N), lambda i: (i, 0, 0))
    masks = [pltpu.VMEM((N, N), F32)] * 3
    maps, inverse, sums, beta, tw = pl.pallas_call(
        maps_kernel,
        grid=(heads // HP,),
        in_specs=[smem, smem, whole(rewards_row.shape), whole(prompts_row.shape), whole(log_gate.shape),
                  whole((heads, depth)), whole(hidden_in.shape)] + [by_heads] * 4,
        out_specs=[square(3), one_square, whole((heads, N)), whole((heads, N)), whole((N, N))],
        out_shape=[jax.ShapeDtypeStruct(s, F32) for s in (
            (heads, 3, N, N), (heads, N, N), (heads, N), (heads, N), (N, N))],
        scratch_shapes=masks,
        compiler_params=params,
        name="segment_maps",
    )(lengths, prompts_row, rewards_row, prompts_row, log_gate, beta_weight.T, hidden_in,
      queries, key_rows, value_rows, out_grad)
    owned = to_owners(maps)
    few_heads = pl.BlockSpec((tokens, HG * N), lambda i: (0, i))
    few_squares = pl.BlockSpec((HG, N, N), lambda i: (i, 0, 0))
    few_parts = pl.BlockSpec((HG, N, 2 * N), lambda i: (i, 0, 0))
    half = jax.ShapeDtypeStruct((heads, N, N), F32)
    in_parts = jax.ShapeDtypeStruct((heads, N, 2 * N), BF16)
    u0, z, dx0, x = pl.pallas_call(
        ahead_kernel,
        grid=(heads // HG,),
        in_specs=[smem] + [few_heads] * 4 + [few_squares, whole((heads, N)), whole((heads, N)), whole((N, N))],
        out_specs=[few_squares, few_parts] * 2,
        out_shape=[half, in_parts] * 2,
        scratch_shapes=masks,
        compiler_params=params,
        cost_estimate=pl.CostEstimate(flops=12_000_000_000, bytes_accessed=40_000_000, transcendentals=0),
        name="ahead",
    )(lengths, queries, key_rows, value_rows, out_grad, inverse, sums, beta, tw)
    ends = pl.pallas_call(
        chains_kernel,
        out_shape=jax.ShapeDtypeStruct((owned.shape[0], 2, N, N), F32),
        in_specs=[pl.BlockSpec(memory_space=pltpu.VMEM)],
        out_specs=pl.BlockSpec(memory_space=pltpu.VMEM),
        compiler_params=pltpu.CompilerParams(vmem_limit_bytes=VMEM_SMALL),
        name="chains",
    )(owned)
    ends = to_owners(ends)
    spread = hidden_in.T.reshape(parts, owned_rows, tokens).transpose(1, 0, 2)
    parts_spec = pl.BlockSpec((HP, N, 2 * N), lambda i: (i, 0, 0))
    u, dx, dw = pl.pallas_call(
        logits_kernel,
        grid=(heads // HP,),
        in_specs=[square(2)] + [one_square, parts_spec] * 2 + [whole((heads, N)), whole(spread.shape)],
        out_specs=[one_square] * 2 + [whole((parts, 1, tiles * N))],
        out_shape=[half] * 2 + [jax.ShapeDtypeStruct((parts, 1, tiles * N), F32)],
        scratch_shapes=[pltpu.VMEM((N, N), F32)],
        compiler_params=params,
        name="logit_grads",
    )(ends, u0, z, dx0, x, beta, spread)
    pieces = lax.all_to_all(dw, ("dp", "ctx"), 0, 0, tiled=True)
    dq, dk, dv, dgate = pl.pallas_call(
        grads_kernel,
        grid=(heads // HG,),
        in_specs=[smem] + [few_heads] * 3 + [pl.BlockSpec((HG, 2, N, N), lambda i: (i, 0, 0, 0)), few_squares, few_squares,
                                             whole((heads, N)), whole((heads, N)), whole((N, N))],
        out_specs=[few_heads] * 3 + [whole((heads, N))],
        out_shape=[jax.ShapeDtypeStruct((tokens, width), BF16)] * 3 + [jax.ShapeDtypeStruct((heads, N), F32)],
        scratch_shapes=masks,
        compiler_params=params,
        cost_estimate=pl.CostEstimate(flops=12_000_000_000, bytes_accessed=40_000_000, transcendentals=0),
        name="segment_grads",
    )(lengths, queries, key_rows, out_grad, ends, u, dx, sums, beta, tw)
    dweight = pl.pallas_call(
        sum_kernel,
        out_shape=jax.ShapeDtypeStruct((heads, owned_rows), F32),
        in_specs=[pl.BlockSpec(memory_space=pltpu.VMEM)],
        out_specs=pl.BlockSpec(memory_space=pltpu.VMEM),
        scratch_shapes=[pltpu.VMEM((N, N), F32)],
        compiler_params=pltpu.CompilerParams(vmem_limit_bytes=VMEM_SMALL),
        name="sum_parts",
    )(pieces)
    return dq, dk, dv, dgate, dweight.T


def solution(mesh):
    rows = P(("dp", "ctx"), None)
    gates = P(None, ("dp", "ctx"))
    in_specs = (rows, rows, rows, rows, P(), gates, rows, P("dp", None), P(), P())
    out_specs = (rows, rows, rows, gates, rows)
    return jax.shard_map(local, mesh=mesh, in_specs=in_specs, out_specs=out_specs, check_vma=False)
```

```python
import jax
import jax.numpy as jnp
from jax import lax
from jax.experimental import pallas as pl
from jax.experimental.pallas import tpu as pltpu
from jax.sharding import PartitionSpec as P

F32 = jnp.float32
BF16 = jnp.bfloat16
N = 128
HP = 8
HG = 4
VMEM_LIMIT = 56 * 1024 * 1024
VMEM_MID = 48 * 1024 * 1024
VMEM_SMALL = 24 * 1024 * 1024
NN = (((1,), (0,)), ((), ()))
NT = (((1,), (1,)), ((), ()))
TN = (((0,), (0,)), ((), ()))


def split(x):
    hi = x.astype(BF16)
    return hi, (x - hi.astype(F32)).astype(BF16)


def dot(a, b, dims):
    return lax.dot_general(a, b, dims, preferred_element_type=F32)


def dot3(a, b, dims):
    return parts_dot(jnp.concatenate(split(a), dims[0][0][0]), b, dims)


def parts_dot(a_parts, b, dims):
    kb = dims[0][1][0]
    n = b.shape[1 - kb]
    rights = jnp.concatenate(split(b), 1 - kb)
    both = dot(a_parts, jnp.concatenate([rights, rights], kb), dims)
    return both[:, :n] + both[:, n:]


def dot2l(a, b, dims):
    (ka,), (kb,) = dims[0]
    return dot(jnp.concatenate(split(a), ka), jnp.concatenate([b, b], kb), dims)


def dot2r(a, b, dims):
    (ka,), (kb,) = dims[0]
    return dot(jnp.concatenate([a, a], ka), jnp.concatenate(split(b), kb), dims)


def iota(axis):
    return lax.broadcasted_iota(jnp.int32, (N, N), axis)


def unit_inverses(lowers):
    rows, cols = iota(0), iota(1)
    same = jnp.where(rows == cols, 1.0, 0.0)
    pair = jnp.where(rows // 2 == cols // 2, 1.0, 0.0)
    inverses = [same - pair * lower for lower in lowers]
    size = 2
    while size < N:
        off = jnp.where((rows // (2 * size) == cols // (2 * size)) & (rows // size != cols // size), 1.0, 0.0)
        steps = [dot3(off * lower, inverse, NN) for lower, inverse in zip(lowers, inverses)]
        inverses = [inverse - dot3(inverse, step, NN) for inverse, step in zip(inverses, steps)]
        size *= 2
    return inverses


def begins_of(lens_ref):
    begins, at = [], jnp.int32(0)
    for i in range(lens_ref.shape[1]):
        begins.append(at)
        at = at + lens_ref[0, i]
    return begins


def plan(lens_ref, ctx):
    begins = begins_of(lens_ref)
    first = ctx * N
    row_pos, col_pos = iota(0) + first, iota(1) + first

    def count(at):
        return sum((b <= at).astype(jnp.int32) for b in begins)

    row_id, col_id = count(row_pos), count(col_pos)
    linked = jnp.where((row_id == col_id) & (row_pos >= col_pos), 1.0, 0.0)
    head = jnp.where(row_id == count(first - 1), 1.0, 0.0)
    tail = jnp.where(row_id == count(first + N - 1), 1.0, 0.0)
    return linked, head, tail, row_id


def token_weights(lens_ref, prompts_ref, rewards_row, prompts_row, row_id, dp):
    rolls = lens_ref.shape[1]
    lanes = lax.broadcasted_iota(jnp.int32, rewards_row.shape, 1)
    weight = jnp.zeros((N, N), F32)
    for i in range(rolls):
        at = dp * rolls + i
        same = jnp.where(prompts_row == prompts_ref[0, at], 1.0, 0.0)
        mean = jnp.sum(same * rewards_row, axis=1, keepdims=True) / jnp.sum(same, axis=1, keepdims=True)
        own = jnp.sum(jnp.where(lanes == at, rewards_row, 0.0), axis=1, keepdims=True)
        length = jnp.full((1, 1), lens_ref[0, i], jnp.int32).astype(F32)
        scale = (own - mean) * (16.0 * N) / (rolls * length)
        weight = jnp.where(row_id == i + 1, scale, weight)
    return weight


def inverse_norm(rows):
    total = jnp.sum(rows * rows, axis=1, keepdims=True)
    return jnp.broadcast_to(lax.rsqrt(total + 1e-06), (N, N))


def by_row(row):
    return jnp.broadcast_to(row, (N, N)).T


def head_terms(q, k, gate_row, beta_row, linked, head, tail):
    qf, kf = q.astype(F32), k.astype(F32)
    rq, rk = inverse_norm(qf), inverse_norm(kf)
    rk_cols = rk.T
    gate = by_row(gate_row)
    decay = jnp.exp(jnp.minimum(gate - gate_row, 0.0)) * linked
    pairs = dot(jnp.concatenate([k, q], axis=0), k, NT)
    key_key = pairs[:N] * rk * rk_cols
    query_key = pairs[N:] * rq * rk_cols
    from_head = head * jnp.exp(gate)
    to_tail = tail * jnp.exp(gate[N - 1 : N, :] - gate)
    return qf * rq, kf * rk, rq, rk, rk_cols, decay, key_key, query_key, from_head, to_tail, by_row(beta_row)


def maps_kernel(lens_ref, prompts_ref, rewards_row_ref, prompts_row_ref, gate_ref, weight_ref, hidden_ref,
                q_ref, k_ref, v_ref, g_ref,
                maps_ref, inv_ref, sum_ref, beta_ref, tw_ref,
                linked_s, head_s, tail_s):
    ctx, dp = lax.axis_index("ctx"), lax.axis_index("dp")

    @pl.when(pl.program_id(0) == 0)
    def _():
        linked, head, tail, row_id = plan(lens_ref, ctx)
        linked_s[...], head_s[...], tail_s[...] = linked, head, tail
        tw_ref[...] = token_weights(lens_ref, prompts_ref, rewards_row_ref[...], prompts_row_ref[...], row_id, dp)
        logits = dot(weight_ref[...], hidden_ref[...], NT)
        beta_ref[...] = 1.0 / (1.0 + jnp.exp(-logits))
        upto = jnp.where(iota(0) <= iota(1), 1.0, 0.0).astype(BF16)
        gates = gate_ref[...]
        hi, rest = split(gates)
        mid = gates - hi.astype(F32)
        mid, low = split(mid)
        sum_ref[...] = dot(hi, upto, NN) + (dot(mid, upto, NN) + dot(low, upto, NN))

    linked, head, tail, tw = linked_s[...], head_s[...], tail_s[...], tw_ref[...]
    strict = jnp.where(iota(0) > iota(1), 1.0, 0.0)
    same = jnp.where(iota(0) == iota(1), 1.0, 0.0)
    lowers, rest, mgs = [], [], []
    for i in range(HP):
        h = pl.program_id(0) * HP + i
        cols = slice(i * N, (i + 1) * N)
        q, k, v, g = q_ref[:, cols], k_ref[:, cols], v_ref[:, cols], g_ref[:, cols]
        gate_row, beta_row = sum_ref[pl.ds(h, 1), :], beta_ref[pl.ds(h, 1), :]
        qn, kn, rq, rk, rk_cols, decay, key_key, query_key, from_head, to_tail, beta = head_terms(
            q, k, gate_row, beta_row, linked, head, tail)
        lowers.append(strict * (beta * decay * key_key))
        mgs.append(dot2l(decay * query_key * tw, g, TN))
        maps_ref[i, 2] = dot2r(g, tw * from_head * qn, TN)
        maps_ref[i, 0] = from_head[N - 1 : N, :] * same
        rest.append((jnp.concatenate([beta * v.astype(F32), beta * from_head * kn], axis=1), to_tail * kn))
    inverses = unit_inverses(lowers)
    for i in range(HP):
        inv_ref[i] = inverses[i]
    uzs = [dot3(inverse, sides, NN) for inverse, (sides, _) in zip(inverses, rest)]
    for i in range(HP):
        ends = dot3(uzs[i], rest[i][1], TN)
        maps_ref[i, 0] -= ends[N:]
        maps_ref[i, 1] = ends[:N]
        maps_ref[i, 2] -= dot3(mgs[i], uzs[i][:, N:], TN)


def chains_kernel(maps_ref, out_ref):
    count = maps_ref.shape[0]
    state = jnp.zeros((N, N), F32)
    grad = jnp.zeros((N, N), F32)
    for j in range(count):
        b = count - 1 - j
        out_ref[j, 0] = state
        out_ref[b, 1] = grad
        if j < count - 1:
            state = dot3(state, maps_ref[j, 0], NN) + maps_ref[j, 1]
            grad = dot3(grad, maps_ref[b, 0], NT) + maps_ref[b, 2]


def ahead_kernel(lens_ref, q_ref, k_ref, v_ref, g_ref, inv_ref, sum_ref, beta_ref, tw_ref,
                 pre_ref,
                 linked_s, head_s, tail_s):
    ctx = lax.axis_index("ctx")

    @pl.when(pl.program_id(0) == 0)
    def _():
        linked_s[...], head_s[...], tail_s[...], unused = plan(lens_ref, ctx)

    linked, head, tail, tw = linked_s[...], head_s[...], tail_s[...], tw_ref[...]
    for i in range(HG):
        h = pl.program_id(0) * HG + i
        cols = slice(i * N, (i + 1) * N)
        q, k, v, g = q_ref[:, cols], k_ref[:, cols], v_ref[:, cols], g_ref[:, cols]
        gate_row, beta_row = sum_ref[pl.ds(h, 1), :], beta_ref[pl.ds(h, 1), :]
        qn, kn, rq, rk, rk_cols, decay, key_key, query_key, from_head, to_tail, beta = head_terms(
            q, k, gate_row, beta_row, linked, head, tail)
        uz = dot3(inv_ref[i], jnp.concatenate([beta * v.astype(F32), beta * from_head * kn], axis=1), NN)
        pre_ref[i, 0], pre_ref[i, 2] = uz[:, :N], uz[:, N:]
        mg = dot2l(decay * query_key * tw, g, TN)
        dxx = dot3(inv_ref[i], jnp.concatenate([mg, to_tail * kn], axis=1), TN)
        pre_ref[i, 1], pre_ref[i, 3] = dxx[:, :N], dxx[:, N:]


def logits_kernel(ends_ref, pre_ref, beta_ref, spread_ref,
                  udx_ref, dw_ref, sums_s):
    @pl.when(pl.program_id(0) == 0)
    def _():
        sums_s[...] = jnp.zeros((N, N), F32)

    sums = sums_s[...]
    for i in range(HP):
        u = pre_ref[i, 0] - dot3(pre_ref[i, 2], ends_ref[i, 0], NT)
        dx = pre_ref[i, 1] + dot3(pre_ref[i, 3], ends_ref[i, 1], NT)
        udx_ref[i, 0], udx_ref[i, 1] = u, dx
        sums = jnp.where(iota(1) == pl.program_id(0) * HP + i, jnp.sum(dx * u, axis=1, keepdims=True), sums)
    sums_s[...] = sums

    @pl.when(pl.program_id(0) == pl.num_programs(0) - 1)
    def _():
        count = beta_ref.shape[0]
        dlogit = sums * (1.0 - jnp.concatenate([beta_ref[...], jnp.zeros((N - count, N), F32)], axis=0).T)
        per = N // count
        rows = spread_ref.shape[0]
        for first in range(0, rows, per):
            total = jnp.zeros((N, N), F32)
            for r in range(first, min(first + per, rows)):
                moved = dlogit if r == first else pltpu.roll(dlogit, count * (r - first), 1)
                total = total + dot2r(spread_ref[r], moved, NN)
            dw_ref[:, 0, first * count : first * count + N] = total


def grads_kernel(lens_ref, q_ref, k_ref, g_ref, ends_ref, udx_ref, sum_ref, beta_ref, tw_ref,
                 dq_ref, dk_ref, dv_ref, dgate_ref,
                 linked_s, head_s, tail_s):
    ctx = lax.axis_index("ctx")

    @pl.when(pl.program_id(0) == 0)
    def _():
        linked_s[...], head_s[...], tail_s[...], unused = plan(lens_ref, ctx)

    linked, head, tail, tw = linked_s[...], head_s[...], tail_s[...], tw_ref[...]
    strict = jnp.where(iota(0) > iota(1), 1.0, 0.0)
    reach = iota(0) >= iota(1)
    last = jnp.where(lax.broadcasted_iota(jnp.int32, (N, 1), 0) == N - 1, 1.0, 0.0)
    for i in range(HG):
        h = pl.program_id(0) * HG + i
        cols = slice(i * N, (i + 1) * N)
        q, k, g = q_ref[:, cols], k_ref[:, cols], g_ref[:, cols]
        gate_row, beta_row = sum_ref[pl.ds(h, 1), :], beta_ref[pl.ds(h, 1), :]
        qn, kn, rq, rk, rk_cols, decay, key_key, query_key, from_head, to_tail, beta = head_terms(
            q, k, gate_row, beta_row, linked, head, tail)
        state, grad, u, dx = ends_ref[i, 0], ends_ref[i, 1], udx_ref[i, 0], udx_ref[i, 1]
        pair = -(strict * beta * decay) * dot3(dx, u, NT)
        dqk = decay * (tw * dot2r(g, u, NT))
        dtail = dot3(u, grad, NN)
        gs = tw * dot2r(g, state, NN)
        dxs = dot3(dx, state, NN)
        both = dot2l(jnp.concatenate([dqk * rk_cols, (pair + pair.T) * rk_cols], axis=0), k, NN)
        dqn = from_head * gs + both[:N]
        dkn = dot2l(dqk * rq, q, TN) + to_tail * dtail - beta * from_head * dxs + both[N:]
        dq_ref[:, cols] = (rq * (dqn - qn * jnp.sum(dqn * qn, axis=1, keepdims=True))).astype(BF16)
        dk_ref[:, cols] = (rk * (dkn - kn * jnp.sum(dkn * kn, axis=1, keepdims=True))).astype(BF16)
        dv_ref[:, cols] = (beta * dx).astype(BF16)
        spread = dqk * query_key + pair * key_key
        tails = jnp.sum(to_tail * dtail * kn, axis=1, keepdims=True)
        heads = jnp.sum(from_head * (gs * qn - beta * dxs * kn), axis=1, keepdims=True)
        through = jnp.sum(from_head[N - 1 : N, :] * jnp.sum(state * grad, axis=0, keepdims=True), axis=1, keepdims=True)
        dgamma = jnp.sum(spread, axis=1, keepdims=True) + heads - tails
        dgamma = dgamma + last * (jnp.sum(tails, axis=0, keepdims=True) + through)
        dgamma = dgamma - by_row(jnp.sum(spread, axis=0, keepdims=True))
        dgate_ref[pl.ds(h, 1), :] = jnp.sum(jnp.where(reach, dgamma, 0.0), axis=0, keepdims=True)


def sum_kernel(parts_ref, out_ref, rows_s):
    heads, rows = out_ref.shape
    total = jnp.sum(parts_ref[:, 0, :], axis=0, keepdims=True)
    rows_s[...] = jnp.zeros((N, N), F32)
    for r in range(rows):
        rows_s[r : r + 1, :heads] = total[:, r * heads : (r + 1) * heads]
    out_ref[...] = rows_s[...].T[:heads, :rows]


def whole(shape):
    return pl.BlockSpec(shape, lambda i: (0,) * len(shape))


def to_owners(x):
    return lax.all_to_all(x, "ctx", 0, 0, tiled=True)


def local(queries, key_rows, value_rows, hidden_in, beta_weight, log_gate, out_grad, lengths, rewards, prompts):
    tokens, width = queries.shape
    depth, heads = beta_weight.shape
    parts = lax.axis_size("dp") * lax.axis_size("ctx")
    owned_rows = depth // parts
    tiles = -(-owned_rows * heads // N)
    smem = pl.BlockSpec(memory_space=pltpu.SMEM)
    by_heads = pl.BlockSpec((tokens, HP * N), lambda i: (0, i))
    params = pltpu.CompilerParams(vmem_limit_bytes=VMEM_LIMIT)
    prompts_row, rewards_row = prompts.reshape(1, -1), rewards.reshape(1, -1)

    def square(n):
        return pl.BlockSpec((HP, n, N, N), lambda i: (i, 0, 0, 0))

    one_square = pl.BlockSpec((HP, N, N), lambda i: (i, 0, 0))
    masks = [pltpu.VMEM((N, N), F32)] * 3
    maps, inverse, sums, beta, tw = pl.pallas_call(
        maps_kernel,
        grid=(heads // HP,),
        in_specs=[smem, smem, whole(rewards_row.shape), whole(prompts_row.shape), whole(log_gate.shape),
                  whole((heads, depth)), whole(hidden_in.shape)] + [by_heads] * 4,
        out_specs=[square(3), one_square, whole((heads, N)), whole((heads, N)), whole((N, N))],
        out_shape=[jax.ShapeDtypeStruct(s, F32) for s in (
            (heads, 3, N, N), (heads, N, N), (heads, N), (heads, N), (N, N))],
        scratch_shapes=masks,
        compiler_params=params,
        name="segment_maps",
    )(lengths, prompts_row, rewards_row, prompts_row, log_gate, beta_weight.T, hidden_in,
      queries, key_rows, value_rows, out_grad)
    owned = to_owners(maps)
    few_heads = pl.BlockSpec((tokens, HG * N), lambda i: (0, i))
    few_squares = pl.BlockSpec((HG, N, N), lambda i: (i, 0, 0))
    few_pre = pl.BlockSpec((HG, 4, N, N), lambda i: (i, 0, 0, 0))
    pre = pl.pallas_call(
        ahead_kernel,
        grid=(heads // HG,),
        in_specs=[smem] + [few_heads] * 4 + [few_squares, whole((heads, N)), whole((heads, N)), whole((N, N))],
        out_specs=few_pre,
        out_shape=jax.ShapeDtypeStruct((heads, 4, N, N), F32),
        scratch_shapes=masks,
        compiler_params=params,
        cost_estimate=pl.CostEstimate(flops=12_000_000_000, bytes_accessed=40_000_000, transcendentals=0),
        name="ahead",
    )(lengths, queries, key_rows, value_rows, out_grad, inverse, sums, beta, tw)
    ends = pl.pallas_call(
        chains_kernel,
        out_shape=jax.ShapeDtypeStruct((owned.shape[0], 2, N, N), F32),
        in_specs=[pl.BlockSpec(memory_space=pltpu.VMEM)],
        out_specs=pl.BlockSpec(memory_space=pltpu.VMEM),
        compiler_params=pltpu.CompilerParams(vmem_limit_bytes=VMEM_SMALL),
        name="chains",
    )(owned)
    ends = to_owners(ends)
    spread = hidden_in.T.reshape(parts, owned_rows, tokens).transpose(1, 0, 2)
    udx, dw = pl.pallas_call(
        logits_kernel,
        grid=(heads // HP,),
        in_specs=[square(2), square(4)] + [whole((heads, N)), whole(spread.shape)],
        out_specs=[square(2)] + [whole((parts, 1, tiles * N))],
        out_shape=[jax.ShapeDtypeStruct((heads, 4, N, N), F32)] + [jax.ShapeDtypeStruct((parts, 1, tiles * N), F32)],
        scratch_shapes=[pltpu.VMEM((N, N), F32)],
        compiler_params=pltpu.CompilerParams(vmem_limit_bytes=VMEM_MID),
        input_output_aliases={1: 0},
        name="logit_grads",
    )(ends, pre, beta, spread)
    pieces = lax.all_to_all(dw, ("dp", "ctx"), 0, 0, tiled=True)
    dq, dk, dv, dgate = pl.pallas_call(
        grads_kernel,
        grid=(heads // HG,),
        in_specs=[smem] + [few_heads] * 3 + [pl.BlockSpec((HG, 2, N, N), lambda i: (i, 0, 0, 0))] * 2 + [
                                             whole((heads, N)), whole((heads, N)), whole((N, N))],
        out_specs=[few_heads] * 3 + [whole((heads, N))],
        out_shape=[jax.ShapeDtypeStruct((tokens, width), BF16)] * 3 + [jax.ShapeDtypeStruct((heads, N), F32)],
        scratch_shapes=masks,
        compiler_params=params,
        cost_estimate=pl.CostEstimate(flops=12_000_000_000, bytes_accessed=40_000_000, transcendentals=0),
        name="segment_grads",
    )(lengths, queries, key_rows, out_grad, ends, udx, sums, beta, tw)
    dweight = pl.pallas_call(
        sum_kernel,
        out_shape=jax.ShapeDtypeStruct((heads, owned_rows), F32),
        in_specs=[pl.BlockSpec(memory_space=pltpu.VMEM)],
        out_specs=pl.BlockSpec(memory_space=pltpu.VMEM),
        scratch_shapes=[pltpu.VMEM((N, N), F32)],
        compiler_params=pltpu.CompilerParams(vmem_limit_bytes=VMEM_SMALL),
        name="sum_parts",
    )(pieces)
    return dq, dk, dv, dgate, dweight.T


def solution(mesh):
    rows = P(("dp", "ctx"), None)
    gates = P(None, ("dp", "ctx"))
    in_specs = (rows, rows, rows, rows, P(), gates, rows, P("dp", None), P(), P())
    out_specs = (rows, rows, rows, gates, rows)
    return jax.shard_map(local, mesh=mesh, in_specs=in_specs, out_specs=out_specs, check_vma=False)
```

```python
import jax
import jax.numpy as jnp
from jax import lax
from jax.experimental import pallas as pl
from jax.experimental.pallas import tpu as pltpu
from jax.sharding import PartitionSpec as P

F32 = jnp.float32
BF16 = jnp.bfloat16
N = 128
HP = 8
HG = 4
VMEM_LIMIT = 56 * 1024 * 1024
VMEM_MID = 48 * 1024 * 1024
VMEM_FIRST = 40 * 1024 * 1024
VMEM_SMALL = 24 * 1024 * 1024
NN = (((1,), (0,)), ((), ()))
NT = (((1,), (1,)), ((), ()))
TN = (((0,), (0,)), ((), ()))


def split(x):
    hi = x.astype(BF16)
    return hi, (x - hi.astype(F32)).astype(BF16)


def dot(a, b, dims):
    return lax.dot_general(a, b, dims, preferred_element_type=F32)


def dot3(a, b, dims):
    return parts_dot(jnp.concatenate(split(a), dims[0][0][0]), b, dims)


def parts_dot(a_parts, b, dims):
    kb = dims[0][1][0]
    n = b.shape[1 - kb]
    rights = jnp.concatenate(split(b), 1 - kb)
    both = dot(a_parts, jnp.concatenate([rights, rights], kb), dims)
    return both[:, :n] + both[:, n:]


def dot2l(a, b, dims):
    (ka,), (kb,) = dims[0]
    return dot(jnp.concatenate(split(a), ka), jnp.concatenate([b, b], kb), dims)


def dot2r(a, b, dims):
    (ka,), (kb,) = dims[0]
    return dot(jnp.concatenate([a, a], ka), jnp.concatenate(split(b), kb), dims)


def iota(axis):
    return lax.broadcasted_iota(jnp.int32, (N, N), axis)


def unit_inverses(lowers):
    rows, cols = iota(0), iota(1)
    same = jnp.where(rows == cols, 1.0, 0.0)
    pair = jnp.where(rows // 2 == cols // 2, 1.0, 0.0)
    inverses = [same - pair * lower for lower in lowers]
    size = 2
    while size < N:
        off = jnp.where((rows // (2 * size) == cols // (2 * size)) & (rows // size != cols // size), 1.0, 0.0)
        steps = [dot3(off * lower, inverse, NN) for lower, inverse in zip(lowers, inverses)]
        inverses = [inverse - dot3(inverse, step, NN) for inverse, step in zip(inverses, steps)]
        size *= 2
    return inverses


def begins_of(lens_ref):
    begins, at = [], jnp.int32(0)
    for i in range(lens_ref.shape[1]):
        begins.append(at)
        at = at + lens_ref[0, i]
    return begins


def plan(lens_ref, ctx):
    begins = begins_of(lens_ref)
    first = ctx * N
    row_pos, col_pos = iota(0) + first, iota(1) + first

    def count(at):
        return sum((b <= at).astype(jnp.int32) for b in begins)

    row_id, col_id = count(row_pos), count(col_pos)
    linked = jnp.where((row_id == col_id) & (row_pos >= col_pos), 1.0, 0.0)
    head = jnp.where(row_id == count(first - 1), 1.0, 0.0)
    tail = jnp.where(row_id == count(first + N - 1), 1.0, 0.0)
    return linked, head, tail, row_id


def token_weights(lens_ref, prompts_ref, rewards_row, prompts_row, row_id, dp):
    rolls = lens_ref.shape[1]
    lanes = lax.broadcasted_iota(jnp.int32, rewards_row.shape, 1)
    weight = jnp.zeros((N, N), F32)
    for i in range(rolls):
        at = dp * rolls + i
        same = jnp.where(prompts_row == prompts_ref[0, at], 1.0, 0.0)
        mean = jnp.sum(same * rewards_row, axis=1, keepdims=True) / jnp.sum(same, axis=1, keepdims=True)
        own = jnp.sum(jnp.where(lanes == at, rewards_row, 0.0), axis=1, keepdims=True)
        length = jnp.full((1, 1), lens_ref[0, i], jnp.int32).astype(F32)
        scale = (own - mean) * (16.0 * N) / (rolls * length)
        weight = jnp.where(row_id == i + 1, scale, weight)
    return weight


def inverse_norm(rows):
    total = jnp.sum(rows * rows, axis=1, keepdims=True)
    return jnp.broadcast_to(lax.rsqrt(total + 1e-06), (N, N))


def by_row(row):
    return jnp.broadcast_to(row, (N, N)).T


def head_terms(q, k, gate_row, beta_row, linked, head, tail):
    qf, kf = q.astype(F32), k.astype(F32)
    rq, rk = inverse_norm(qf), inverse_norm(kf)
    rk_cols = rk.T
    gate = by_row(gate_row)
    decay = jnp.exp(jnp.minimum(gate - gate_row, 0.0)) * linked
    pairs = dot(jnp.concatenate([k, q], axis=0), k, NT)
    key_key = pairs[:N] * rk * rk_cols
    query_key = pairs[N:] * rq * rk_cols
    from_head = head * jnp.exp(gate)
    to_tail = tail * jnp.exp(gate[N - 1 : N, :] - gate)
    return qf * rq, kf * rk, rq, rk, rk_cols, decay, key_key, query_key, from_head, to_tail, by_row(beta_row)


def maps_kernel(lens_ref, prompts_ref, rewards_row_ref, prompts_row_ref, gate_ref, weight_ref, hidden_ref,
                q_ref, k_ref, v_ref, g_ref,
                maps_ref, inv_ref, sum_ref, beta_ref, tw_ref,
                linked_s, head_s, tail_s):
    ctx, dp = lax.axis_index("ctx"), lax.axis_index("dp")

    @pl.when(pl.program_id(0) == 0)
    def _():
        linked, head, tail, row_id = plan(lens_ref, ctx)
        linked_s[...], head_s[...], tail_s[...] = linked, head, tail
        tw_ref[...] = token_weights(lens_ref, prompts_ref, rewards_row_ref[...], prompts_row_ref[...], row_id, dp)
        logits = dot(weight_ref[...], hidden_ref[...], NT)
        beta_ref[...] = 1.0 / (1.0 + jnp.exp(-logits))
        upto = jnp.where(iota(0) <= iota(1), 1.0, 0.0).astype(BF16)
        gates = gate_ref[...]
        hi, rest = split(gates)
        mid = gates - hi.astype(F32)
        mid, low = split(mid)
        sum_ref[...] = dot(hi, upto, NN) + (dot(mid, upto, NN) + dot(low, upto, NN))

    linked, head, tail, tw = linked_s[...], head_s[...], tail_s[...], tw_ref[...]
    strict = jnp.where(iota(0) > iota(1), 1.0, 0.0)
    same = jnp.where(iota(0) == iota(1), 1.0, 0.0)
    lowers, rest, mgs = [], [], []
    for i in range(HP):
        h = pl.program_id(0) * HP + i
        cols = slice(i * N, (i + 1) * N)
        q, k, v, g = q_ref[:, cols], k_ref[:, cols], v_ref[:, cols], g_ref[:, cols]
        gate_row, beta_row = sum_ref[pl.ds(h, 1), :], beta_ref[pl.ds(h, 1), :]
        qn, kn, rq, rk, rk_cols, decay, key_key, query_key, from_head, to_tail, beta = head_terms(
            q, k, gate_row, beta_row, linked, head, tail)
        lowers.append(strict * (beta * decay * key_key))
        mgs.append(dot2l(decay * query_key * tw, g, TN))
        maps_ref[i, 2] = dot2r(g, tw * from_head * qn, TN)
        maps_ref[i, 0] = from_head[N - 1 : N, :] * same
        rest.append((jnp.concatenate([beta * v.astype(F32), beta * from_head * kn], axis=1), to_tail * kn))
    inverses = unit_inverses(lowers)
    for i in range(HP):
        inv_ref[i] = inverses[i]
    uzs = [dot3(inverse, sides, NN) for inverse, (sides, _) in zip(inverses, rest)]
    for i in range(HP):
        ends = dot3(uzs[i], rest[i][1], TN)
        maps_ref[i, 0] -= ends[N:]
        maps_ref[i, 1] = ends[:N]
        maps_ref[i, 2] -= dot3(mgs[i], uzs[i][:, N:], TN)


def chains_kernel(maps_ref, out_ref):
    count = maps_ref.shape[0]
    state = jnp.zeros((N, N), F32)
    grad = jnp.zeros((N, N), F32)
    for j in range(count):
        b = count - 1 - j
        out_ref[j, 0] = state
        out_ref[b, 1] = grad
        if j < count - 1:
            state = dot3(state, maps_ref[j, 0], NN) + maps_ref[j, 1]
            grad = dot3(grad, maps_ref[b, 0], NT) + maps_ref[b, 2]


def ahead_kernel(lens_ref, q_ref, k_ref, v_ref, g_ref, inv_ref, sum_ref, beta_ref, tw_ref,
                 pre_ref,
                 linked_s, head_s, tail_s):
    ctx = lax.axis_index("ctx")

    @pl.when(pl.program_id(0) == 0)
    def _():
        linked_s[...], head_s[...], tail_s[...], unused = plan(lens_ref, ctx)

    linked, head, tail, tw = linked_s[...], head_s[...], tail_s[...], tw_ref[...]
    for i in range(HG):
        h = pl.program_id(0) * HG + i
        cols = slice(i * N, (i + 1) * N)
        q, k, v, g = q_ref[:, cols], k_ref[:, cols], v_ref[:, cols], g_ref[:, cols]
        gate_row, beta_row = sum_ref[pl.ds(h, 1), :], beta_ref[pl.ds(h, 1), :]
        qn, kn, rq, rk, rk_cols, decay, key_key, query_key, from_head, to_tail, beta = head_terms(
            q, k, gate_row, beta_row, linked, head, tail)
        uz = dot3(inv_ref[i], jnp.concatenate([beta * v.astype(F32), beta * from_head * kn], axis=1), NN)
        pre_ref[i, 0], pre_ref[i, 2] = uz[:, :N], uz[:, N:]
        mg = dot2l(decay * query_key * tw, g, TN)
        dxx = dot3(inv_ref[i], jnp.concatenate([mg, to_tail * kn], axis=1), TN)
        pre_ref[i, 1], pre_ref[i, 3] = dxx[:, :N], dxx[:, N:]


def logits_kernel(ends_ref, pre_ref, beta_ref, spread_ref,
                  udx_ref, dw_ref, sums_s):
    @pl.when(pl.program_id(0) == 0)
    def _():
        sums_s[...] = jnp.zeros((N, N), F32)

    sums = sums_s[...]
    for i in range(HP):
        u = pre_ref[i, 0] - dot3(pre_ref[i, 2], ends_ref[i, 0], NT)
        dx = pre_ref[i, 1] + dot3(pre_ref[i, 3], ends_ref[i, 1], NT)
        udx_ref[i, 0], udx_ref[i, 1] = u, dx
        sums = jnp.where(iota(1) == pl.program_id(0) * HP + i, jnp.sum(dx * u, axis=1, keepdims=True), sums)
    sums_s[...] = sums

    @pl.when(pl.program_id(0) == pl.num_programs(0) - 1)
    def _():
        count = beta_ref.shape[0]
        dlogit = sums * (1.0 - jnp.concatenate([beta_ref[...], jnp.zeros((N - count, N), F32)], axis=0).T)
        per = N // count
        rows = spread_ref.shape[0]
        for first in range(0, rows, per):
            total = jnp.zeros((N, N), F32)
            for r in range(first, min(first + per, rows)):
                moved = dlogit if r == first else pltpu.roll(dlogit, count * (r - first), 1)
                total = total + dot2r(spread_ref[r], moved, NN)
            dw_ref[:, 0, first * count : first * count + N] = total


def grads_kernel(lens_ref, q_ref, k_ref, g_ref, ends_ref, udx_ref, sum_ref, beta_ref, tw_ref,
                 dq_ref, dk_ref, dv_ref, dgate_ref,
                 linked_s, head_s, tail_s):
    ctx = lax.axis_index("ctx")

    @pl.when(pl.program_id(0) == 0)
    def _():
        linked_s[...], head_s[...], tail_s[...], unused = plan(lens_ref, ctx)

    linked, head, tail, tw = linked_s[...], head_s[...], tail_s[...], tw_ref[...]
    strict = jnp.where(iota(0) > iota(1), 1.0, 0.0)
    reach = iota(0) >= iota(1)
    last = jnp.where(lax.broadcasted_iota(jnp.int32, (N, 1), 0) == N - 1, 1.0, 0.0)
    for i in range(HG):
        h = pl.program_id(0) * HG + i
        cols = slice(i * N, (i + 1) * N)
        q, k, g = q_ref[:, cols], k_ref[:, cols], g_ref[:, cols]
        gate_row, beta_row = sum_ref[pl.ds(h, 1), :], beta_ref[pl.ds(h, 1), :]
        qn, kn, rq, rk, rk_cols, decay, key_key, query_key, from_head, to_tail, beta = head_terms(
            q, k, gate_row, beta_row, linked, head, tail)
        state, grad, u, dx = ends_ref[i, 0], ends_ref[i, 1], udx_ref[i, 0], udx_ref[i, 1]
        pair = -(strict * beta * decay) * dot3(dx, u, NT)
        dqk = decay * (tw * dot2r(g, u, NT))
        dtail = dot3(u, grad, NN)
        gs = tw * dot2r(g, state, NN)
        dxs = dot3(dx, state, NN)
        both = dot2l(jnp.concatenate([dqk * rk_cols, (pair + pair.T) * rk_cols], axis=0), k, NN)
        dqn = from_head * gs + both[:N]
        dkn = dot2l(dqk * rq, q, TN) + to_tail * dtail - beta * from_head * dxs + both[N:]
        dq_ref[:, cols] = (rq * (dqn - qn * jnp.sum(dqn * qn, axis=1, keepdims=True))).astype(BF16)
        dk_ref[:, cols] = (rk * (dkn - kn * jnp.sum(dkn * kn, axis=1, keepdims=True))).astype(BF16)
        dv_ref[:, cols] = (beta * dx).astype(BF16)
        spread = dqk * query_key + pair * key_key
        tails = jnp.sum(to_tail * dtail * kn, axis=1, keepdims=True)
        heads = jnp.sum(from_head * (gs * qn - beta * dxs * kn), axis=1, keepdims=True)
        through = jnp.sum(from_head[N - 1 : N, :] * jnp.sum(state * grad, axis=0, keepdims=True), axis=1, keepdims=True)
        dgamma = jnp.sum(spread, axis=1, keepdims=True) + heads - tails
        dgamma = dgamma + last * (jnp.sum(tails, axis=0, keepdims=True) + through)
        dgamma = dgamma - by_row(jnp.sum(spread, axis=0, keepdims=True))
        dgate_ref[pl.ds(h, 1), :] = jnp.sum(jnp.where(reach, dgamma, 0.0), axis=0, keepdims=True)


def sum_kernel(parts_ref, out_ref, rows_s):
    heads, rows = out_ref.shape
    total = jnp.sum(parts_ref[:, 0, :], axis=0, keepdims=True)
    rows_s[...] = jnp.zeros((N, N), F32)
    for r in range(rows):
        rows_s[r : r + 1, :heads] = total[:, r * heads : (r + 1) * heads]
    out_ref[...] = rows_s[...].T[:heads, :rows]


def whole(shape):
    return pl.BlockSpec(shape, lambda i: (0,) * len(shape))


def to_owners(x):
    return lax.all_to_all(x, "ctx", 0, 0, tiled=True)


def local(queries, key_rows, value_rows, hidden_in, beta_weight, log_gate, out_grad, lengths, rewards, prompts):
    tokens, width = queries.shape
    depth, heads = beta_weight.shape
    parts = lax.axis_size("dp") * lax.axis_size("ctx")
    owned_rows = depth // parts
    tiles = -(-owned_rows * heads // N)
    smem = pl.BlockSpec(memory_space=pltpu.SMEM)
    by_heads = pl.BlockSpec((tokens, HP * N), lambda i: (0, i))
    params = pltpu.CompilerParams(vmem_limit_bytes=VMEM_LIMIT)
    prompts_row, rewards_row = prompts.reshape(1, -1), rewards.reshape(1, -1)

    def square(n):
        return pl.BlockSpec((HP, n, N, N), lambda i: (i, 0, 0, 0))

    one_square = pl.BlockSpec((HP, N, N), lambda i: (i, 0, 0))
    masks = [pltpu.VMEM((N, N), F32)] * 3
    maps, inverse, sums, beta, tw = pl.pallas_call(
        maps_kernel,
        grid=(heads // HP,),
        in_specs=[smem, smem, whole(rewards_row.shape), whole(prompts_row.shape), whole(log_gate.shape),
                  whole((heads, depth)), whole(hidden_in.shape)] + [by_heads] * 4,
        out_specs=[square(3), one_square, whole((heads, N)), whole((heads, N)), whole((N, N))],
        out_shape=[jax.ShapeDtypeStruct(s, F32) for s in (
            (heads, 3, N, N), (heads, N, N), (heads, N), (heads, N), (N, N))],
        scratch_shapes=masks,
        compiler_params=pltpu.CompilerParams(vmem_limit_bytes=VMEM_FIRST),
        name="segment_maps",
    )(lengths, prompts_row, rewards_row, prompts_row, log_gate, beta_weight.T, hidden_in,
      queries, key_rows, value_rows, out_grad)
    owned = to_owners(maps)
    few_heads = pl.BlockSpec((tokens, HG * N), lambda i: (0, i))
    few_squares = pl.BlockSpec((HG, N, N), lambda i: (i, 0, 0))
    few_pre = pl.BlockSpec((HG, 4, N, N), lambda i: (i, 0, 0, 0))
    pre = pl.pallas_call(
        ahead_kernel,
        grid=(heads // HG,),
        in_specs=[smem] + [few_heads] * 4 + [few_squares, whole((heads, N)), whole((heads, N)), whole((N, N))],
        out_specs=few_pre,
        out_shape=jax.ShapeDtypeStruct((heads, 4, N, N), F32),
        scratch_shapes=masks,
        compiler_params=params,
        cost_estimate=pl.CostEstimate(flops=12_000_000_000, bytes_accessed=40_000_000, transcendentals=0),
        name="ahead",
    )(lengths, queries, key_rows, value_rows, out_grad, inverse, sums, beta, tw)
    ends = pl.pallas_call(
        chains_kernel,
        out_shape=jax.ShapeDtypeStruct((owned.shape[0], 2, N, N), F32),
        in_specs=[pl.BlockSpec(memory_space=pltpu.VMEM)],
        out_specs=pl.BlockSpec(memory_space=pltpu.VMEM),
        compiler_params=pltpu.CompilerParams(vmem_limit_bytes=VMEM_SMALL),
        name="chains",
    )(owned)
    ends = to_owners(ends)
    spread = hidden_in.T.reshape(parts, owned_rows, tokens).transpose(1, 0, 2)
    udx, dw = pl.pallas_call(
        logits_kernel,
        grid=(heads // HP,),
        in_specs=[square(2), square(4)] + [whole((heads, N)), whole(spread.shape)],
        out_specs=[square(2)] + [whole((parts, 1, tiles * N))],
        out_shape=[jax.ShapeDtypeStruct((heads, 4, N, N), F32)] + [jax.ShapeDtypeStruct((parts, 1, tiles * N), F32)],
        scratch_shapes=[pltpu.VMEM((N, N), F32)],
        compiler_params=pltpu.CompilerParams(vmem_limit_bytes=VMEM_MID),
        input_output_aliases={1: 0},
        name="logit_grads",
    )(ends, pre, beta, spread)
    pieces = lax.all_to_all(dw, ("dp", "ctx"), 0, 0, tiled=True)
    dq, dk, dv, dgate = pl.pallas_call(
        grads_kernel,
        grid=(heads // HG,),
        in_specs=[smem] + [few_heads] * 3 + [pl.BlockSpec((HG, 2, N, N), lambda i: (i, 0, 0, 0))] * 2 + [
                                             whole((heads, N)), whole((heads, N)), whole((N, N))],
        out_specs=[few_heads] * 3 + [whole((heads, N))],
        out_shape=[jax.ShapeDtypeStruct((tokens, width), BF16)] * 3 + [jax.ShapeDtypeStruct((heads, N), F32)],
        scratch_shapes=masks,
        compiler_params=params,
        cost_estimate=pl.CostEstimate(flops=12_000_000_000, bytes_accessed=40_000_000, transcendentals=0),
        name="segment_grads",
    )(lengths, queries, key_rows, out_grad, ends, udx, sums, beta, tw)
    dweight = pl.pallas_call(
        sum_kernel,
        out_shape=jax.ShapeDtypeStruct((heads, owned_rows), F32),
        in_specs=[pl.BlockSpec(memory_space=pltpu.VMEM)],
        out_specs=pl.BlockSpec(memory_space=pltpu.VMEM),
        scratch_shapes=[pltpu.VMEM((N, N), F32)],
        compiler_params=pltpu.CompilerParams(vmem_limit_bytes=VMEM_SMALL),
        name="sum_parts",
    )(pieces)
    return dq, dk, dv, dgate, dweight.T


def solution(mesh):
    rows = P(("dp", "ctx"), None)
    gates = P(None, ("dp", "ctx"))
    in_specs = (rows, rows, rows, rows, P(), gates, rows, P("dp", None), P(), P())
    out_specs = (rows, rows, rows, gates, rows)
    return jax.shard_map(local, mesh=mesh, in_specs=in_specs, out_specs=out_specs, check_vma=False)
```

```python
import jax
import jax.numpy as jnp
from jax import lax
from jax.experimental import pallas as pl
from jax.experimental.pallas import tpu as pltpu
from jax.sharding import PartitionSpec as P

F32 = jnp.float32
BF16 = jnp.bfloat16
N = 128
HP = 8
HG = 4
VMEM_LIMIT = 56 * 1024 * 1024
VMEM_MID = 48 * 1024 * 1024
VMEM_SMALL = 24 * 1024 * 1024
NN = (((1,), (0,)), ((), ()))
NT = (((1,), (1,)), ((), ()))
TN = (((0,), (0,)), ((), ()))


def split(x):
    hi = x.astype(BF16)
    return hi, (x - hi.astype(F32)).astype(BF16)


def dot(a, b, dims):
    return lax.dot_general(a, b, dims, preferred_element_type=F32)


def dot3(a, b, dims):
    return parts_dot(jnp.concatenate(split(a), dims[0][0][0]), b, dims)


def parts_dot(a_parts, b, dims):
    kb = dims[0][1][0]
    n = b.shape[1 - kb]
    rights = jnp.concatenate(split(b), 1 - kb)
    both = dot(a_parts, jnp.concatenate([rights, rights], kb), dims)
    return both[:, :n] + both[:, n:]


def dot2l(a, b, dims):
    (ka,), (kb,) = dims[0]
    return dot(jnp.concatenate(split(a), ka), jnp.concatenate([b, b], kb), dims)


def dot2r(a, b, dims):
    (ka,), (kb,) = dims[0]
    return dot(jnp.concatenate([a, a], ka), jnp.concatenate(split(b), kb), dims)


def iota(axis):
    return lax.broadcasted_iota(jnp.int32, (N, N), axis)


def unit_inverses(lowers):
    rows, cols = iota(0), iota(1)
    same = jnp.where(rows == cols, 1.0, 0.0)
    pair = jnp.where(rows // 2 == cols // 2, 1.0, 0.0)
    inverses = [same - pair * lower for lower in lowers]
    size = 2
    while size < N:
        off = jnp.where((rows // (2 * size) == cols // (2 * size)) & (rows // size != cols // size), 1.0, 0.0)
        steps = [dot3(off * lower, inverse, NN) for lower, inverse in zip(lowers, inverses)]
        inverses = [inverse - dot3(inverse, step, NN) for inverse, step in zip(inverses, steps)]
        size *= 2
    return inverses


def begins_of(lens_ref):
    begins, at = [], jnp.int32(0)
    for i in range(lens_ref.shape[1]):
        begins.append(at)
        at = at + lens_ref[0, i]
    return begins


def plan(lens_ref, ctx):
    begins = begins_of(lens_ref)
    first = ctx * N
    row_pos, col_pos = iota(0) + first, iota(1) + first

    def count(at):
        return sum((b <= at).astype(jnp.int32) for b in begins)

    row_id, col_id = count(row_pos), count(col_pos)
    linked = jnp.where((row_id == col_id) & (row_pos >= col_pos), 1.0, 0.0)
    head = jnp.where(row_id == count(first - 1), 1.0, 0.0)
    tail = jnp.where(row_id == count(first + N - 1), 1.0, 0.0)
    return linked, head, tail, row_id


def token_weights(lens_ref, prompts_ref, rewards_row, prompts_row, row_id, dp):
    rolls = lens_ref.shape[1]
    lanes = lax.broadcasted_iota(jnp.int32, rewards_row.shape, 1)
    weight = jnp.zeros((N, N), F32)
    for i in range(rolls):
        at = dp * rolls + i
        same = jnp.where(prompts_row == prompts_ref[0, at], 1.0, 0.0)
        mean = jnp.sum(same * rewards_row, axis=1, keepdims=True) / jnp.sum(same, axis=1, keepdims=True)
        own = jnp.sum(jnp.where(lanes == at, rewards_row, 0.0), axis=1, keepdims=True)
        length = jnp.full((1, 1), lens_ref[0, i], jnp.int32).astype(F32)
        scale = (own - mean) * (16.0 * N) / (rolls * length)
        weight = jnp.where(row_id == i + 1, scale, weight)
    return weight


def inverse_norm(rows):
    total = jnp.sum(rows * rows, axis=1, keepdims=True)
    return jnp.broadcast_to(lax.rsqrt(total + 1e-06), (N, N))


def by_row(row):
    return jnp.broadcast_to(row, (N, N)).T


def head_terms(q, k, gate_row, beta_row, linked, head, tail):
    qf, kf = q.astype(F32), k.astype(F32)
    rq, rk = inverse_norm(qf), inverse_norm(kf)
    rk_cols = rk.T
    gate = by_row(gate_row)
    decay = jnp.exp(jnp.minimum(gate - gate_row, 0.0)) * linked
    pairs = dot(jnp.concatenate([k, q], axis=0), k, NT)
    key_key = pairs[:N] * rk * rk_cols
    query_key = pairs[N:] * rq * rk_cols
    from_head = head * jnp.exp(gate)
    to_tail = tail * jnp.exp(gate[N - 1 : N, :] - gate)
    return qf * rq, kf * rk, rq, rk, rk_cols, decay, key_key, query_key, from_head, to_tail, by_row(beta_row)


def maps_kernel(lens_ref, prompts_ref, rewards_row_ref, prompts_row_ref, gate_ref, weight_ref, hidden_ref,
                q_ref, k_ref, v_ref, g_ref,
                maps_ref, sum_ref, beta_ref, tw_ref,
                linked_s, head_s, tail_s):
    ctx, dp = lax.axis_index("ctx"), lax.axis_index("dp")

    @pl.when(pl.program_id(0) == 0)
    def _():
        linked, head, tail, row_id = plan(lens_ref, ctx)
        linked_s[...], head_s[...], tail_s[...] = linked, head, tail
        tw_ref[...] = token_weights(lens_ref, prompts_ref, rewards_row_ref[...], prompts_row_ref[...], row_id, dp)
        logits = dot(weight_ref[...], hidden_ref[...], NT)
        beta_ref[...] = 1.0 / (1.0 + jnp.exp(-logits))
        upto = jnp.where(iota(0) <= iota(1), 1.0, 0.0).astype(BF16)
        gates = gate_ref[...]
        hi, rest = split(gates)
        mid = gates - hi.astype(F32)
        mid, low = split(mid)
        sum_ref[...] = dot(hi, upto, NN) + (dot(mid, upto, NN) + dot(low, upto, NN))

    linked, head, tail, tw = linked_s[...], head_s[...], tail_s[...], tw_ref[...]
    strict = jnp.where(iota(0) > iota(1), 1.0, 0.0)
    same = jnp.where(iota(0) == iota(1), 1.0, 0.0)
    lowers, rest, mgs = [], [], []
    for i in range(HP):
        h = pl.program_id(0) * HP + i
        cols = slice(i * N, (i + 1) * N)
        q, k, v, g = q_ref[:, cols], k_ref[:, cols], v_ref[:, cols], g_ref[:, cols]
        gate_row, beta_row = sum_ref[pl.ds(h, 1), :], beta_ref[pl.ds(h, 1), :]
        qn, kn, rq, rk, rk_cols, decay, key_key, query_key, from_head, to_tail, beta = head_terms(
            q, k, gate_row, beta_row, linked, head, tail)
        lowers.append(strict * (beta * decay * key_key))
        mgs.append(dot2l(decay * query_key * tw, g, TN))
        maps_ref[i, 2] = dot2r(g, tw * from_head * qn, TN)
        maps_ref[i, 0] = from_head[N - 1 : N, :] * same
        rest.append((jnp.concatenate([beta * v.astype(F32), beta * from_head * kn], axis=1), to_tail * kn))
    inverses = unit_inverses(lowers)
    uzs = [dot3(inverse, sides, NN) for inverse, (sides, _) in zip(inverses, rest)]
    for i in range(HP):
        ends = dot3(uzs[i], rest[i][1], TN)
        maps_ref[i, 0] -= ends[N:]
        maps_ref[i, 1] = ends[:N]
        maps_ref[i, 2] -= dot3(mgs[i], uzs[i][:, N:], TN)


def chains_kernel(maps_ref, out_ref):
    count = maps_ref.shape[0]
    state = jnp.zeros((N, N), F32)
    grad = jnp.zeros((N, N), F32)
    for j in range(count):
        b = count - 1 - j
        out_ref[j, 0] = state
        out_ref[b, 1] = grad
        if j < count - 1:
            state = dot3(state, maps_ref[j, 0], NN) + maps_ref[j, 1]
            grad = dot3(grad, maps_ref[b, 0], NT) + maps_ref[b, 2]


def ahead_kernel(lens_ref, q_ref, k_ref, v_ref, g_ref, sum_ref, beta_ref, tw_ref,
                 pre_ref,
                 linked_s, head_s, tail_s):
    ctx = lax.axis_index("ctx")

    @pl.when(pl.program_id(0) == 0)
    def _():
        linked_s[...], head_s[...], tail_s[...], unused = plan(lens_ref, ctx)

    linked, head, tail, tw = linked_s[...], head_s[...], tail_s[...], tw_ref[...]
    strict = jnp.where(iota(0) > iota(1), 1.0, 0.0)
    lowers, lefts, rights = [], [], []
    for i in range(HG):
        h = pl.program_id(0) * HG + i
        cols = slice(i * N, (i + 1) * N)
        q, k, v, g = q_ref[:, cols], k_ref[:, cols], v_ref[:, cols], g_ref[:, cols]
        gate_row, beta_row = sum_ref[pl.ds(h, 1), :], beta_ref[pl.ds(h, 1), :]
        qn, kn, rq, rk, rk_cols, decay, key_key, query_key, from_head, to_tail, beta = head_terms(
            q, k, gate_row, beta_row, linked, head, tail)
        lowers.append(strict * (beta * decay * key_key))
        lefts.append(jnp.concatenate([beta * v.astype(F32), beta * from_head * kn], axis=1))
        rights.append(jnp.concatenate([dot2l(decay * query_key * tw, g, TN), to_tail * kn], axis=1))
    inverses = unit_inverses(lowers)
    for i in range(HG):
        uz = dot3(inverses[i], lefts[i], NN)
        dxx = dot3(inverses[i], rights[i], TN)
        pre_ref[i, 0], pre_ref[i, 2] = uz[:, :N], uz[:, N:]
        pre_ref[i, 1], pre_ref[i, 3] = dxx[:, :N], dxx[:, N:]


def logits_kernel(ends_ref, pre_ref, beta_ref, spread_ref,
                  udx_ref, dw_ref, sums_s):
    @pl.when(pl.program_id(0) == 0)
    def _():
        sums_s[...] = jnp.zeros((N, N), F32)

    sums = sums_s[...]
    for i in range(HP):
        u = pre_ref[i, 0] - dot3(pre_ref[i, 2], ends_ref[i, 0], NT)
        dx = pre_ref[i, 1] + dot3(pre_ref[i, 3], ends_ref[i, 1], NT)
        udx_ref[i, 0], udx_ref[i, 1] = u, dx
        sums = jnp.where(iota(1) == pl.program_id(0) * HP + i, jnp.sum(dx * u, axis=1, keepdims=True), sums)
    sums_s[...] = sums

    @pl.when(pl.program_id(0) == pl.num_programs(0) - 1)
    def _():
        count = beta_ref.shape[0]
        dlogit = sums * (1.0 - jnp.concatenate([beta_ref[...], jnp.zeros((N - count, N), F32)], axis=0).T)
        per = N // count
        rows = spread_ref.shape[0]
        for first in range(0, rows, per):
            total = jnp.zeros((N, N), F32)
            for r in range(first, min(first + per, rows)):
                moved = dlogit if r == first else pltpu.roll(dlogit, count * (r - first), 1)
                total = total + dot2r(spread_ref[r], moved, NN)
            dw_ref[:, 0, first * count : first * count + N] = total


def grads_kernel(lens_ref, q_ref, k_ref, g_ref, ends_ref, udx_ref, sum_ref, beta_ref, tw_ref,
                 dq_ref, dk_ref, dv_ref, dgate_ref,
                 linked_s, head_s, tail_s):
    ctx = lax.axis_index("ctx")

    @pl.when(pl.program_id(0) == 0)
    def _():
        linked_s[...], head_s[...], tail_s[...], unused = plan(lens_ref, ctx)

    linked, head, tail, tw = linked_s[...], head_s[...], tail_s[...], tw_ref[...]
    strict = jnp.where(iota(0) > iota(1), 1.0, 0.0)
    reach = iota(0) >= iota(1)
    last = jnp.where(lax.broadcasted_iota(jnp.int32, (N, 1), 0) == N - 1, 1.0, 0.0)
    for i in range(HG):
        h = pl.program_id(0) * HG + i
        cols = slice(i * N, (i + 1) * N)
        q, k, g = q_ref[:, cols], k_ref[:, cols], g_ref[:, cols]
        gate_row, beta_row = sum_ref[pl.ds(h, 1), :], beta_ref[pl.ds(h, 1), :]
        qn, kn, rq, rk, rk_cols, decay, key_key, query_key, from_head, to_tail, beta = head_terms(
            q, k, gate_row, beta_row, linked, head, tail)
        state, grad, u, dx = ends_ref[i, 0], ends_ref[i, 1], udx_ref[i, 0], udx_ref[i, 1]
        pair = -(strict * beta * decay) * dot3(dx, u, NT)
        dqk = decay * (tw * dot2r(g, u, NT))
        dtail = dot3(u, grad, NN)
        gs = tw * dot2r(g, state, NN)
        dxs = dot3(dx, state, NN)
        both = dot2l(jnp.concatenate([dqk * rk_cols, (pair + pair.T) * rk_cols], axis=0), k, NN)
        dqn = from_head * gs + both[:N]
        dkn = dot2l(dqk * rq, q, TN) + to_tail * dtail - beta * from_head * dxs + both[N:]
        dq_ref[:, cols] = (rq * (dqn - qn * jnp.sum(dqn * qn, axis=1, keepdims=True))).astype(BF16)
        dk_ref[:, cols] = (rk * (dkn - kn * jnp.sum(dkn * kn, axis=1, keepdims=True))).astype(BF16)
        dv_ref[:, cols] = (beta * dx).astype(BF16)
        spread = dqk * query_key + pair * key_key
        tails = jnp.sum(to_tail * dtail * kn, axis=1, keepdims=True)
        heads = jnp.sum(from_head * (gs * qn - beta * dxs * kn), axis=1, keepdims=True)
        through = jnp.sum(from_head[N - 1 : N, :] * jnp.sum(state * grad, axis=0, keepdims=True), axis=1, keepdims=True)
        dgamma = jnp.sum(spread, axis=1, keepdims=True) + heads - tails
        dgamma = dgamma + last * (jnp.sum(tails, axis=0, keepdims=True) + through)
        dgamma = dgamma - by_row(jnp.sum(spread, axis=0, keepdims=True))
        dgate_ref[pl.ds(h, 1), :] = jnp.sum(jnp.where(reach, dgamma, 0.0), axis=0, keepdims=True)


def sum_kernel(parts_ref, out_ref, rows_s):
    heads, rows = out_ref.shape
    total = jnp.sum(parts_ref[:, 0, :], axis=0, keepdims=True)
    rows_s[...] = jnp.zeros((N, N), F32)
    for r in range(rows):
        rows_s[r : r + 1, :heads] = total[:, r * heads : (r + 1) * heads]
    out_ref[...] = rows_s[...].T[:heads, :rows]


def whole(shape):
    return pl.BlockSpec(shape, lambda i: (0,) * len(shape))


def to_owners(x):
    return lax.all_to_all(x, "ctx", 0, 0, tiled=True)


def local(queries, key_rows, value_rows, hidden_in, beta_weight, log_gate, out_grad, lengths, rewards, prompts):
    tokens, width = queries.shape
    depth, heads = beta_weight.shape
    parts = lax.axis_size("dp") * lax.axis_size("ctx")
    owned_rows = depth // parts
    tiles = -(-owned_rows * heads // N)
    smem = pl.BlockSpec(memory_space=pltpu.SMEM)
    by_heads = pl.BlockSpec((tokens, HP * N), lambda i: (0, i))
    params = pltpu.CompilerParams(vmem_limit_bytes=VMEM_LIMIT)
    prompts_row, rewards_row = prompts.reshape(1, -1), rewards.reshape(1, -1)

    def square(n):
        return pl.BlockSpec((HP, n, N, N), lambda i: (i, 0, 0, 0))

    one_square = pl.BlockSpec((HP, N, N), lambda i: (i, 0, 0))
    masks = [pltpu.VMEM((N, N), F32)] * 3
    maps, sums, beta, tw = pl.pallas_call(
        maps_kernel,
        grid=(heads // HP,),
        in_specs=[smem, smem, whole(rewards_row.shape), whole(prompts_row.shape), whole(log_gate.shape),
                  whole((heads, depth)), whole(hidden_in.shape)] + [by_heads] * 4,
        out_specs=[square(3), whole((heads, N)), whole((heads, N)), whole((N, N))],
        out_shape=[jax.ShapeDtypeStruct(s, F32) for s in (
            (heads, 3, N, N), (heads, N), (heads, N), (N, N))],
        scratch_shapes=masks,
        compiler_params=params,
        name="segment_maps",
    )(lengths, prompts_row, rewards_row, prompts_row, log_gate, beta_weight.T, hidden_in,
      queries, key_rows, value_rows, out_grad)
    owned = to_owners(maps)
    few_heads = pl.BlockSpec((tokens, HG * N), lambda i: (0, i))
    few_squares = pl.BlockSpec((HG, N, N), lambda i: (i, 0, 0))
    few_pre = pl.BlockSpec((HG, 4, N, N), lambda i: (i, 0, 0, 0))
    pre = pl.pallas_call(
        ahead_kernel,
        grid=(heads // HG,),
        in_specs=[smem] + [few_heads] * 4 + [whole((heads, N)), whole((heads, N)), whole((N, N))],
        out_specs=few_pre,
        out_shape=jax.ShapeDtypeStruct((heads, 4, N, N), F32),
        scratch_shapes=masks,
        compiler_params=params,
        cost_estimate=pl.CostEstimate(flops=12_000_000_000, bytes_accessed=40_000_000, transcendentals=0),
        name="ahead",
    )(lengths, queries, key_rows, value_rows, out_grad, sums, beta, tw)
    ends = pl.pallas_call(
        chains_kernel,
        out_shape=jax.ShapeDtypeStruct((owned.shape[0], 2, N, N), F32),
        in_specs=[pl.BlockSpec(memory_space=pltpu.VMEM)],
        out_specs=pl.BlockSpec(memory_space=pltpu.VMEM),
        compiler_params=pltpu.CompilerParams(vmem_limit_bytes=VMEM_SMALL),
        name="chains",
    )(owned)
    ends = to_owners(ends)
    spread = hidden_in.T.reshape(parts, owned_rows, tokens).transpose(1, 0, 2)
    udx, dw = pl.pallas_call(
        logits_kernel,
        grid=(heads // HP,),
        in_specs=[square(2), square(4)] + [whole((heads, N)), whole(spread.shape)],
        out_specs=[square(2)] + [whole((parts, 1, tiles * N))],
        out_shape=[jax.ShapeDtypeStruct((heads, 4, N, N), F32)] + [jax.ShapeDtypeStruct((parts, 1, tiles * N), F32)],
        scratch_shapes=[pltpu.VMEM((N, N), F32)],
        compiler_params=pltpu.CompilerParams(vmem_limit_bytes=VMEM_MID),
        input_output_aliases={1: 0},
        name="logit_grads",
    )(ends, pre, beta, spread)
    pieces = lax.all_to_all(dw, ("dp", "ctx"), 0, 0, tiled=True)
    dq, dk, dv, dgate = pl.pallas_call(
        grads_kernel,
        grid=(heads // HG,),
        in_specs=[smem] + [few_heads] * 3 + [pl.BlockSpec((HG, 2, N, N), lambda i: (i, 0, 0, 0))] * 2 + [
                                             whole((heads, N)), whole((heads, N)), whole((N, N))],
        out_specs=[few_heads] * 3 + [whole((heads, N))],
        out_shape=[jax.ShapeDtypeStruct((tokens, width), BF16)] * 3 + [jax.ShapeDtypeStruct((heads, N), F32)],
        scratch_shapes=masks,
        compiler_params=params,
        cost_estimate=pl.CostEstimate(flops=12_000_000_000, bytes_accessed=40_000_000, transcendentals=0),
        name="segment_grads",
    )(lengths, queries, key_rows, out_grad, ends, udx, sums, beta, tw)
    dweight = pl.pallas_call(
        sum_kernel,
        out_shape=jax.ShapeDtypeStruct((heads, owned_rows), F32),
        in_specs=[pl.BlockSpec(memory_space=pltpu.VMEM)],
        out_specs=pl.BlockSpec(memory_space=pltpu.VMEM),
        scratch_shapes=[pltpu.VMEM((N, N), F32)],
        compiler_params=pltpu.CompilerParams(vmem_limit_bytes=VMEM_SMALL),
        name="sum_parts",
    )(pieces)
    return dq, dk, dv, dgate, dweight.T


def solution(mesh):
    rows = P(("dp", "ctx"), None)
    gates = P(None, ("dp", "ctx"))
    in_specs = (rows, rows, rows, rows, P(), gates, rows, P("dp", None), P(), P())
    out_specs = (rows, rows, rows, gates, rows)
    return jax.shard_map(local, mesh=mesh, in_specs=in_specs, out_specs=out_specs, check_vma=False)
```
